512 devices in a mesh: dp: 32 (over x, y, core), seq: 16 (over z).
Axes of the slice: x: 4, y: 4, z: 16, core: 2. Of those that a mesh axis runs over, the one named last changes fastest.
Arguments:
- query_rows: bfloat16 [64, 1024, 2048], P('dp', 'seq'), may hold values from -6.5 to 6.5
- key_rows: bfloat16 [64, 1024, 2048], P('dp', 'seq'), may hold values from -6.5 to 6.5
- value_rows: bfloat16 [64, 1024, 2048], P('dp', 'seq'), may hold values from -6 to 6
- cotangent: bfloat16 [64, 1024, 2048], P('dp', 'seq'), may hold values from -6 to 6
- segment_ids: int32 [64, 1024], P('dp', 'seq'), may hold values from 0 to 15, as said below
- moved_slot: int32 [32], P('dp'), may hold values from 0 to 2, as said below
- query_gain: float32 [32, 64], P('seq'), may hold values from 0.5 to 5.6
- key_gain: float32 [32, 64], P('seq'), may hold values from 0.5 to 5.6
Outputs:
- attended: bfloat16 [64, 1024, 2048], P('dp', 'seq')
- grad_queries: bfloat16 [64, 1024, 2048], P('dp', 'seq')
- grad_keys: bfloat16 [64, 1024, 2048], P('dp', 'seq')
- grad_values: bfloat16 [64, 1024, 2048], P('dp', 'seq')
- grad_query_gain: float32 [32, 64], P('seq', 'dp')
- grad_key_gain: float32 [32, 64], P('seq', 'dp')
The draws below stay inside these ranges and needn't reach their ends.
Inputs may be any that keep to these rules, and one draw needn't show every extreme that they name: `segment_ids`: within a pack the ids start at 0 and never fall; every image spans a whole multiple of 64 patches on a multiple of 64; some pack is a single image of 1024 patches. `moved_slot`: group g and group g xor 16 hold the same value; the value 2 means that no pack is traded, any other value s that the packs in slot s of the two groups trade places.
All inputs are finite; a program needn't handle non-finite values.
Results may differ from the reference program's by a relative error of at most 0.011.
The reference program's roundings to bfloat16 on the way (of `query_norm`, `key_norm`, `weights_low` and `score_grad`) count: a program that leaves them out, or rounds other values in their place, can miss the bound.
Values may be sent and summed in bfloat16 or wider, within the bound.
A program may use at most 64 MiB of HBM per device.

```python
import math
from functools import partial
import jax
import jax.numpy as jnp
from jax import lax

HEADS = 32
HEAD_DIM = 64
PACK_LEN = 1024
NPK = 2
IMG_UNIT = 64
PACKS = 64
N_DP = 32


def drawn_rows(key):
    return jax.random.normal(key, (PACKS, PACK_LEN, HEADS * HEAD_DIM), jnp.float32)


def draw_query_rows(key, part):
    shared = drawn_rows(key)
    key = jax.random.fold_in(key, 5)
    return jnp.clip(jax.random.normal(key, shared.shape, jnp.float32), -6.0, 6.0).astype(jnp.bfloat16)


def draw_key_rows(key, part):
    shared = drawn_rows(key)
    key = jax.random.fold_in(key, 7)
    return jnp.clip(jax.random.normal(key, shared.shape, jnp.float32), -6.0, 6.0).astype(jnp.bfloat16)


def draw_query_gain(key, part):
    key = jax.random.fold_in(key, 13)
    return jnp.exp(jax.random.uniform(key, (HEADS, HEAD_DIM), jnp.float32, math.log(0.5), math.log(2.0)))


def draw_key_gain(key, part):
    key = jax.random.fold_in(key, 17)
    return jnp.exp(jax.random.uniform(key, (HEADS, HEAD_DIM), jnp.float32, math.log(0.5), math.log(2.0)))


def draw_segment_ids(key, part):
    key = jax.random.fold_in(key, 11)
    first, second = jax.random.split(key)
    unit_count = PACK_LEN // IMG_UNIT
    cut_level = jax.random.randint(first, (PACKS, 1), 0, 8)
    boundary = (jax.random.randint(second, (PACKS, unit_count - 1), 0, 8) < cut_level).astype(jnp.int32)
    pack_row = jnp.arange(PACKS)[:, None]
    boundary = jnp.where(pack_row == 0, 0, jnp.where(pack_row == 1, 1, boundary))
    unit_ids = jnp.concatenate([jnp.zeros((PACKS, 1), jnp.int32), jnp.cumsum(boundary, axis=1).astype(jnp.int32)], axis=1)
    return jnp.repeat(unit_ids, IMG_UNIT, axis=1).astype(jnp.int32)


def draw_moved_slot(key, part):
    key = jax.random.fold_in(key, 23)
    first, second = jax.random.split(key)
    pair_count = N_DP // 2
    pair_slots = jax.random.randint(first, (pair_count,), 0, NPK + 1)
    forced = jax.random.randint(second, (pair_count,), 0, NPK)
    pair_index = jnp.arange(pair_count)
    pair_slots = jnp.where(pair_index == 0, forced, jnp.where(pair_index == 1, NPK, pair_slots))
    return jnp.concatenate([pair_slots, pair_slots]).astype(jnp.int32)


def block_scale(stream_key, extent, cuts, low, top_value):
    level, own = 1.0, jax.random.fold_in(stream_key, 6)
    for dim, shards_of in cuts:
        heights = jnp.exp(jax.random.uniform(jax.random.fold_in(own, dim), (shards_of,), jnp.float32, low / len(cuts), top_value / len(cuts)))
        level = level * jnp.repeat(heights, extent[dim] // shards_of).reshape([-1 if axis == dim else 1 for axis in range(len(extent))])
    return level


def bell_draw(stream_key, shape, spread, bound, cuts=(), kind=jnp.bfloat16):
    loudness = block_scale(stream_key, shape, cuts, -0.22, 0.18) if cuts else 1.0
    array = jax.random.normal(stream_key, shape, jnp.float32) * spread * loudness
    return jnp.minimum(jnp.maximum(array, -bound), bound).astype(kind)


def setup_inputs(seed: int = 0) -> dict:
    seeds = jax.random.split(jax.random.key(seed), 9)
    query_rows = draw_query_rows(jax.random.fold_in(seeds[8], 71), 0)
    key_rows = draw_key_rows(jax.random.fold_in(seeds[8], 71), 0)
    value_rows = bell_draw(seeds[2], (PACKS, PACK_LEN, HEADS * HEAD_DIM), 1.0, 6.0, ((0, 32), (1, 16)))
    cotangent = bell_draw(seeds[3], (PACKS, PACK_LEN, HEADS * HEAD_DIM), 1.0, 6.0, ((0, 32), (1, 16)))
    segment_ids = draw_segment_ids(jax.random.fold_in(seeds[8], 71), 0)
    moved_slot = draw_moved_slot(jax.random.fold_in(seeds[8], 71), 0)
    query_gain = draw_query_gain(jax.random.fold_in(seeds[8], 71), 0)
    key_gain = draw_key_gain(jax.random.fold_in(seeds[8], 71), 0)
    return {"query_rows": query_rows, "key_rows": key_rows, "value_rows": value_rows, "cotangent": cotangent, "segment_ids": segment_ids, "moved_slot": moved_slot, "query_gain": query_gain, "key_gain": key_gain}


EPSILON = 1e-06

def normalize(raw, gain):
    average = lax.optimization_barrier(jnp.mean(raw, axis=-1, keepdims=True))
    centred = raw - average
    inv_std = lax.rsqrt(lax.optimization_barrier(jnp.mean(centred * centred, axis=-1, keepdims=True)) + EPSILON)
    unit_rows = centred * inv_std
    return (unit_rows, inv_std, (unit_rows * gain).astype(jnp.bfloat16))

def norm_back(grad, unit_rows, inv_std, gain):
    scaled = grad * gain
    inner = scaled - lax.optimization_barrier(jnp.mean(scaled, axis=-1, keepdims=True)) - unit_rows * lax.optimization_barrier(jnp.mean(scaled * unit_rows, axis=-1, keepdims=True))
    return ((inv_std * inner).astype(jnp.bfloat16), lax.optimization_barrier(jnp.sum(grad * unit_rows, axis=0)))

def widen(low):
    return lax.optimization_barrier(low).astype(jnp.float32)

def pack_work(query_gain, key_gain, pieces):
    query_part, key_part, value_part, cot_part, seg_part = pieces
    row_shape = (PACK_LEN, HEADS, HEAD_DIM)
    score_scale = HEAD_DIM ** (-0.5)
    query_unit, query_scale, query_norm = normalize(query_part.astype(jnp.float32).reshape(row_shape), query_gain)
    key_unit, key_scale, key_norm = normalize(key_part.astype(jnp.float32).reshape(row_shape), key_gain)
    query_wide = widen(query_norm)
    key_wide = widen(key_norm)
    value_wide = value_part.astype(jnp.float32).reshape(row_shape)
    cot_wide = cot_part.astype(jnp.float32).reshape(row_shape)
    high = lax.Precision.HIGHEST
    scores = jnp.einsum('qhd,khd->hqk', query_wide, key_wide, precision=high) * score_scale
    same = seg_part[:, None] == seg_part[None, :]
    scores = jnp.where(same[None], scores, -jnp.inf)
    row_max = lax.optimization_barrier(jnp.max(scores, axis=-1, keepdims=True))
    exponent = jnp.exp(scores - row_max)
    weights = exponent / lax.optimization_barrier(jnp.sum(exponent, axis=-1, keepdims=True))
    weights_low = widen(weights.astype(jnp.bfloat16))
    attended_full = jnp.einsum('hqk,khd->qhd', weights_low, value_wide, precision=high)
    row_delta = lax.optimization_barrier(jnp.sum(cot_wide * attended_full, axis=-1))
    prob_grad = jnp.einsum('qhd,khd->hqk', cot_wide, value_wide, precision=high)
    score_grad = widen((weights * (prob_grad - jnp.transpose(row_delta)[:, :, None])).astype(jnp.bfloat16))
    grad_values = jnp.einsum('hqk,qhd->khd', weights_low, cot_wide, precision=high)
    norm_query_grad = jnp.einsum('hqk,khd->qhd', score_grad, key_wide, precision=high) * score_scale
    norm_key_grad = jnp.einsum('hqk,qhd->khd', score_grad, query_wide, precision=high) * score_scale
    grad_queries, gain_query = norm_back(norm_query_grad, query_unit, query_scale, query_gain)
    grad_keys, gain_key = norm_back(norm_key_grad, key_unit, key_scale, key_gain)
    flat = (PACK_LEN, HEADS * HEAD_DIM)
    return (attended_full.astype(jnp.bfloat16).reshape(flat), grad_queries.reshape(flat), grad_keys.reshape(flat), grad_values.astype(jnp.bfloat16).reshape(flat), gain_query, gain_key)

def reference(query_rows, key_rows, value_rows, cotangent, segment_ids, moved_slot, query_gain, key_gain):
    slot_ids = jnp.arange(PACKS, dtype=jnp.int32)
    group_ids = slot_ids // NPK
    within = slot_ids % NPK
    partner = jnp.bitwise_xor(group_ids, N_DP // 2)
    source = jnp.where(moved_slot[group_ids] == within, partner * NPK + within, slot_ids).astype(jnp.int32)
    gathered = (jnp.take(query_rows, source, axis=0), jnp.take(key_rows, source, axis=0), jnp.take(value_rows, source, axis=0), jnp.take(cotangent, source, axis=0), jnp.take(segment_ids, source, axis=0))
    results = lax.map(partial(pack_work, query_gain, key_gain), gathered)
    attended, grad_queries, grad_keys, grad_values, gain_query, gain_key = results
    return (attended, grad_queries, grad_keys, grad_values, lax.optimization_barrier(jnp.sum(gain_query, axis=0)), lax.optimization_barrier(jnp.sum(gain_key, axis=0)))
```

```python
import functools

import jax
import jax.numpy as jnp
from jax import lax
from jax.experimental import pallas as pl
from jax.experimental.pallas import tpu as pltpu
from jax.sharding import PartitionSpec as P

MESH = pl.DeviceIdType.MESH
HEAD_DIM = 64
EPSILON = 1e-06
ROWS = 64
LANES = 128
SCALE = HEAD_DIM ** (-0.5)
MASKED = -1e30
F32 = jnp.float32
BF16 = jnp.bfloat16


def dot(a, b):
    return jnp.dot(a, b, preferred_element_type=F32)


def column(gain):
    row = jnp.concatenate([gain[0:1, :], gain[1:2, :]], axis=1)
    return jnp.transpose(jnp.broadcast_to(row, (LANES, LANES)))[:, 0:1]


def normalize(raw):
    parts = raw.reshape(2, HEAD_DIM, raw.shape[1])
    centred = parts - jnp.mean(parts, axis=1, keepdims=True)
    inv_std = lax.rsqrt(jnp.mean(centred * centred, axis=1, keepdims=True) + EPSILON)
    return (centred * inv_std).reshape(raw.shape), inv_std


def norm_back(grad, unit_rows, inv_std, gain):
    scaled = (grad * gain).reshape(2, HEAD_DIM, grad.shape[1])
    unit = unit_rows.reshape(scaled.shape)
    inner = (
        scaled
        - jnp.mean(scaled, axis=1, keepdims=True)
        - unit * jnp.mean(scaled * unit, axis=1, keepdims=True)
    )
    return (inv_std * inner).reshape(grad.shape)


def fold_lanes(x):
    total = x[:, 0:LANES]
    for start in range(LANES, x.shape[1], LANES):
        total = total + x[:, start : start + LANES]
    return total


def main_kernel(
    nz, ndp, block,
    moved_ref, q_ref, k_ref, v_ref, c_ref, seg_ref, qg_ref, kg_ref,
    ab_ref, gain_ref,
    raw, stage, xrecv, inbuf, outbuf,
    seg_stage, seg_x, seg_all,
    q_unit, k_unit, q_inv, k_inv, q_t, c_t, q_n, c_n, k_n, k_t, v_t, seg_col, seg_row,
    key_acc, value_acc, gain_acc, gain_send, gain_recv,
    load_sem, xs, xr, xsegs, xsegr, zs, zr, segs, segr, outs, outr, gs, gr,
):
    dp, z = lax.axis_index("dp"), lax.axis_index("seq")
    length = nz * ROWS
    lanes = nz * LANES
    partner = lax.rem(dp + ndp // 2, ndp)

    def remote(src, dst, send, recv, device):
        return pltpu.make_async_remote_copy(
            src_ref=src, dst_ref=dst, send_sem=send, recv_sem=recv,
            device_id=device, device_id_type=MESH,
        )

    def arrived(ref, sem):
        pltpu.make_async_copy(ref, ref, sem).wait()

    loads = [
        pltpu.make_async_copy(ref, raw.at[a], load_sem.at[a])
        for a, ref in enumerate((q_ref, k_ref, v_ref, c_ref))
    ]
    for load in loads:
        load.start()

    barrier = pltpu.get_barrier_semaphore()
    for d in range(1, nz):
        pl.semaphore_signal(
            barrier, inc=1, device_id=(dp, lax.rem(z + d, nz)), device_id_type=MESH
        )
    for d in range(1, ndp):
        pl.semaphore_signal(
            barrier, inc=1, device_id=(lax.rem(dp + d, ndp), z), device_id_type=MESH
        )
    pl.semaphore_wait(barrier, nz - 1 + ndp - 1)

    by_distance = sorted(range(1, nz), key=lambda d: (min(d, nz - d), d))

    def send_rows(p, slot):
        for d in by_distance:
            peer = lax.rem(z + d, nz)
            remote(
                stage.at[slot, :, :, pl.ds(pl.multiple_of(peer * LANES, LANES), LANES)],
                inbuf.at[p, :, pl.ds(pl.multiple_of(z * ROWS, ROWS), ROWS), :],
                zs.at[p], zr.at[p], (dp, peer),
            ).start()
        pltpu.make_async_copy(
            stage.at[slot, :, :, pl.ds(pl.multiple_of(z * LANES, LANES), LANES)],
            inbuf.at[p, :, pl.ds(pl.multiple_of(z * ROWS, ROWS), ROWS), :],
            zr.at[p],
        ).start()
        seg_all[p, z] = seg_stage[slot]
        for d in by_distance:
            remote(
                seg_stage.at[slot], seg_all.at[p, z], segs.at[p], segr.at[p],
                (dp, lax.rem(z + d, nz)),
            ).start()

    def send_results(p):
        for d in by_distance:
            peer = lax.rem(z + d, nz)
            remote(
                outbuf.at[p, :, pl.ds(pl.multiple_of(peer * ROWS, ROWS), ROWS), :],
                ab_ref.at[p, :, :, pl.ds(pl.multiple_of(z * LANES, LANES), LANES)],
                outs.at[p], outr.at[p], (dp, peer),
            ).start()
        pltpu.make_async_copy(
            outbuf.at[p, :, pl.ds(pl.multiple_of(z * ROWS, ROWS), ROWS), :],
            ab_ref.at[p, :, :, pl.ds(pl.multiple_of(z * LANES, LANES), LANES)],
            outr.at[p],
        ).start()

    moved = moved_ref[0]
    b_first = moved == 0
    segs_in = seg_ref[...].astype(F32)
    seg0 = jnp.broadcast_to(segs_in[0:1, 0:1], (8, LANES))
    seg1 = jnp.broadcast_to(segs_in[1:2, 0:1], (8, LANES))
    seg_stage[0] = jnp.where(b_first, seg1, seg0)
    seg_stage[1] = jnp.where(b_first, seg0, seg1)
    for a, load in enumerate(loads):
        load.wait()
        stage[1, a] = jnp.where(b_first, raw[a, 0], raw[a, 1])
        stage[0, a] = jnp.where(b_first, raw[a, 1], raw[a, 0])
    send_rows(0, 0)
    trades = []
    for a in range(4):
        trade = remote(stage.at[1, a], xrecv.at[a], xs.at[a], xr.at[a], (partner, z))
        trade.start()
        trades.append(trade)
    seg_trade = remote(seg_stage.at[1], seg_x, xsegs, xsegr, (partner, z))
    seg_trade.start()

    stays = moved == 2
    seg_trade.wait()
    seg_stage[2] = jnp.where(stays, seg_stage[1], seg_x[...])
    for a in range(4):
        trades[a].wait()
        stage[2, a] = jnp.where(stays, stage[1, a], xrecv[a])
    send_rows(1, 2)

    q_gain, k_gain = column(qg_ref[...]), column(kg_ref[...])
    gain_acc[...] = jnp.zeros_like(gain_acc)

    def compute(p):
        top = lax.broadcasted_iota(jnp.int32, (LANES, length), 0) < HEAD_DIM
        left = lax.broadcasted_iota(jnp.int32, (length, LANES), 1) < HEAD_DIM

        def split_down(x):
            return jnp.where(top, x, 0.0).astype(BF16), jnp.where(top, 0.0, x).astype(BF16)

        def split_across(x):
            return jnp.where(left, x, 0.0).astype(BF16), jnp.where(left, 0.0, x).astype(BF16)

        ids = seg_all[p, :, 0:1, :]
        spread = jnp.broadcast_to(ids, (nz, ROWS, LANES)).reshape(length, LANES)
        seg_col[...] = spread
        seg_row[...] = jnp.transpose(spread)[0:8, :]

        unit, inv = normalize(jnp.transpose(inbuf[p, 0].astype(F32)))
        q_unit[...], q_inv[...] = unit, inv
        low = (unit * q_gain).astype(BF16).astype(F32) * SCALE
        q_t[0], q_t[1] = split_down(low)
        q_n[0], q_n[1] = split_across(jnp.transpose(low))

        unit, inv = normalize(jnp.transpose(inbuf[p, 1].astype(F32)))
        k_unit[...], k_inv[...] = unit, inv
        low = (unit * k_gain).astype(BF16).astype(F32)
        k_t[...] = low.astype(BF16)
        k_n[...] = jnp.transpose(low).astype(BF16)

        v_t[...] = jnp.transpose(inbuf[p, 2].astype(F32)).astype(BF16)
        cot = inbuf[p, 3].astype(F32)
        c_n[0], c_n[1] = split_across(cot)
        c_t[0], c_t[1] = split_down(jnp.transpose(cot))
        key_acc[...] = jnp.zeros_like(key_acc)
        value_acc[...] = jnp.zeros_like(value_acc)

        def step(i, carry):
            at = pl.ds(pl.multiple_of(i * block, block), block)
            wide = jnp.concatenate([seg_col[...]] * (block // LANES), axis=1)
            same = wide == seg_row[0:1, at]
            attended, grad = [], []
            for h in range(2):
                head = pl.ds(h * HEAD_DIM, HEAD_DIM)
                scores = jnp.where(same, dot(k_n[...], q_t[h, :, at]), MASKED)
                exponent = jnp.exp(scores - jnp.max(scores, axis=0, keepdims=True))
                weights = exponent * (1.0 / jnp.sum(exponent, axis=0, keepdims=True))
                weights_low = weights.astype(BF16)
                full = dot(v_t[head, :], weights_low)
                delta = jnp.sum(c_t[h, head, at].astype(F32) * full, axis=0, keepdims=True)
                prob_grad = dot(inbuf[p, 2], c_t[h, :, at])
                score_grad = (weights * (prob_grad - delta)).astype(BF16)
                value_acc[...] += dot(weights_low, c_n[h, at, :])
                key_acc[...] += dot(score_grad, q_n[h, at, :])
                attended.append(full)
                grad.append(dot(k_t[head, :], score_grad) * SCALE)
            outbuf[p, 0, at, :] = jnp.transpose(jnp.concatenate(attended, axis=0)).astype(BF16)
            grad = jnp.concatenate(grad, axis=0)
            unit = q_unit[:, at]
            gain_acc[0] += fold_lanes(grad * unit)
            back = norm_back(grad, unit, q_inv[:, :, at], q_gain)
            outbuf[p, 1, at, :] = jnp.transpose(back).astype(BF16)
            return carry

        lax.fori_loop(0, length // block, step, 0)
        outbuf[p, 3] = value_acc[...].astype(BF16)
        grad = jnp.transpose(key_acc[...])
        unit = k_unit[...]
        gain_acc[1] += fold_lanes(grad * unit)
        back = norm_back(grad, unit, k_inv[...], k_gain)
        outbuf[p, 2] = jnp.transpose(back).astype(BF16)

    for p in range(2):
        arrived(inbuf.at[p], zr.at[p])
        arrived(seg_all.at[p, pl.ds(0, nz - 1)], segr.at[p])
        compute(p)
        send_results(p)

    rows = [jnp.sum(jnp.transpose(gain_acc[i]), axis=0, keepdims=True) for i in range(2)]
    pick = lax.broadcasted_iota(jnp.int32, (8, LANES), 0)
    gain_send[...] = jnp.where(pick == 0, rows[0], jnp.where(pick == 1, rows[1], 0.0))
    gain_recv[dp] = gain_send[...]
    for d in range(1, ndp):
        remote(gain_send, gain_recv.at[dp], gs, gr, (lax.rem(dp + d, ndp), z)).start()
    arrived(gain_recv.at[pl.ds(0, ndp - 1)], gr)
    gain_ref[...] = jnp.sum(gain_recv[...], axis=0)

    for p in range(2):
        arrived(ab_ref.at[p], outr.at[p])
        arrived(stage.at[2 * p, :, :, pl.ds(0, lanes - LANES)], zs.at[p])
        arrived(seg_all.at[p, pl.ds(0, nz - 1)], segs.at[p])
        arrived(outbuf.at[p, :, pl.ds(0, length - ROWS), :], outs.at[p])
    arrived(gain_recv.at[pl.ds(0, ndp - 1)], gs)


def place_kernel(moved_ref, ab_ref, gain_ref, out0, out1, out2, out3, gq_ref, gk_ref, sem):
    dp = lax.axis_index("dp")
    b_slot = jnp.where(moved_ref[0] == 0, 0, 1)
    copies = []
    for a, out in enumerate((out0, out1, out2, out3)):
        for p in range(2):
            slot = 1 - b_slot if p == 0 else b_slot
            copies.append(pltpu.make_async_copy(ab_ref.at[p, a], out.at[slot], sem.at[a, p]))
            copies[-1].start()
    lane = lax.broadcasted_iota(jnp.int32, (1, LANES), 1)
    down = lax.broadcasted_iota(jnp.int32, (2, 2), 0)
    across = lax.broadcasted_iota(jnp.int32, (2, 2), 1)
    for i, ref in enumerate((gq_ref, gk_ref)):
        row = gain_ref[i : i + 1, :]
        total = jnp.zeros((2, 2), F32)
        for h in range(2):
            for j in range(2):
                chosen = lane == h * HEAD_DIM + 2 * dp + j
                value = jnp.sum(jnp.where(chosen, row, 0.0), axis=1, keepdims=True)
                total = jnp.where((down == h) & (across == j), value, total)
        ref[...] = total
    for copy in copies:
        copy.wait()


def body(nz, ndp, q, k, v, c, seg, moved, q_gain, k_gain):
    length, lanes = nz * ROWS, nz * LANES
    block = min(256, length)
    anywhere = pl.BlockSpec(memory_space=pl.ANY)
    vmem = pl.BlockSpec(memory_space=pltpu.VMEM)
    smem = pl.BlockSpec(memory_space=pltpu.SMEM)
    dma = pltpu.SemaphoreType.DMA
    ab, gains = pl.pallas_call(
        functools.partial(main_kernel, nz, ndp, block),
        out_shape=(
            jax.ShapeDtypeStruct((2, 4, ROWS, lanes), BF16),
            jax.ShapeDtypeStruct((8, LANES), F32),
        ),
        in_specs=[smem] + [anywhere] * 4 + [vmem] * 3,
        out_specs=(anywhere, vmem),
        scratch_shapes=[
            pltpu.VMEM((4, 2, ROWS, lanes), BF16),
            pltpu.VMEM((3, 4, ROWS, lanes), BF16),
            pltpu.VMEM((4, ROWS, lanes), BF16),
            pltpu.VMEM((2, 4, length, LANES), BF16),
            pltpu.VMEM((2, 4, length, LANES), BF16),
            pltpu.VMEM((3, 8, LANES), F32),
            pltpu.VMEM((8, LANES), F32),
            pltpu.VMEM((2, nz, 8, LANES), F32),
            pltpu.VMEM((LANES, length), F32),
            pltpu.VMEM((LANES, length), F32),
            pltpu.VMEM((2, 1, length), F32),
            pltpu.VMEM((2, 1, length), F32),
            pltpu.VMEM((2, LANES, length), BF16),
            pltpu.VMEM((2, LANES, length), BF16),
            pltpu.VMEM((2, length, LANES), BF16),
            pltpu.VMEM((2, length, LANES), BF16),
            pltpu.VMEM((length, LANES), BF16),
            pltpu.VMEM((LANES, length), BF16),
            pltpu.VMEM((LANES, length), BF16),
            pltpu.VMEM((length, LANES), F32),
            pltpu.VMEM((8, length), F32),
            pltpu.VMEM((length, LANES), F32),
            pltpu.VMEM((length, LANES), F32),
            pltpu.VMEM((2, LANES, LANES), F32),
            pltpu.VMEM((8, LANES), F32),
            pltpu.VMEM((ndp, 8, LANES), F32),
            dma((4,)),
            dma((4,)), dma((4,)), dma(()), dma(()),
            dma((2,)), dma((2,)), dma((2,)), dma((2,)),
            dma((2,)), dma((2,)), dma(()), dma(()),
        ],
        compiler_params=pltpu.CompilerParams(
            collective_id=0, has_side_effects=True, vmem_limit_bytes=48 << 20
        ),
        name="attend",
    )(moved, q, k, v, c, seg, q_gain, k_gain)
    rows = jax.ShapeDtypeStruct((2, ROWS, lanes), BF16)
    small = jax.ShapeDtypeStruct((2, 2), F32)
    return pl.pallas_call(
        place_kernel,
        out_shape=(rows, rows, rows, rows, small, small),
        in_specs=[smem, anywhere, vmem],
        out_specs=(anywhere,) * 4 + (vmem, vmem),
        scratch_shapes=[dma((4, 2))],
        name="place",
    )(moved, ab, gains)


def solution(mesh):
    return jax.shard_map(
        functools.partial(body, mesh.shape["seq"], mesh.shape["dp"]),
        mesh=mesh,
        in_specs=(
            P("dp", "seq", None),
            P("dp", "seq", None),
            P("dp", "seq", None),
            P("dp", "seq", None),
            P("dp", "seq"),
            P("dp"),
            P("seq", None),
            P("seq", None),
        ),
        out_specs=(
            P("dp", "seq", None),
            P("dp", "seq", None),
            P("dp", "seq", None),
            P("dp", "seq", None),
            P("seq", "dp"),
            P("seq", "dp"),
        ),
        check_vma=False,
    )
```

```python
import functools

import jax
import jax.numpy as jnp
from jax import lax
from jax.experimental import pallas as pl
from jax.experimental.pallas import tpu as pltpu
from jax.sharding import PartitionSpec as P

MESH = pl.DeviceIdType.MESH
HEAD_DIM = 64
EPSILON = 1e-06
ROWS = 64
LANES = 128
SCALE = HEAD_DIM ** (-0.5)
MASKED = -1e30
F32 = jnp.float32
BF16 = jnp.bfloat16


def dot(a, b):
    return jnp.dot(a, b, preferred_element_type=F32)


def column(gain):
    row = jnp.concatenate([gain[0:1, :], gain[1:2, :]], axis=1)
    return jnp.transpose(jnp.broadcast_to(row, (LANES, LANES)))[:, 0:1]


def normalize(raw):
    parts = raw.reshape(2, HEAD_DIM, raw.shape[1])
    centred = parts - jnp.mean(parts, axis=1, keepdims=True)
    inv_std = lax.rsqrt(jnp.mean(centred * centred, axis=1, keepdims=True) + EPSILON)
    return (centred * inv_std).reshape(raw.shape), inv_std


def norm_back(grad, unit_rows, inv_std, gain):
    scaled = (grad * gain).reshape(2, HEAD_DIM, grad.shape[1])
    unit = unit_rows.reshape(scaled.shape)
    inner = (
        scaled
        - jnp.mean(scaled, axis=1, keepdims=True)
        - unit * jnp.mean(scaled * unit, axis=1, keepdims=True)
    )
    return (inv_std * inner).reshape(grad.shape)


def fold_lanes(x):
    total = x[:, 0:LANES]
    for start in range(LANES, x.shape[1], LANES):
        total = total + x[:, start : start + LANES]
    return total


def main_kernel(
    nz, ndp, block,
    moved_ref, q_ref, k_ref, v_ref, c_ref, seg_hbm, qg_hbm, kg_hbm,
    ab_ref, gain_ref,
    raw, seg_ref, qg_ref, kg_ref, stage, xrecv, inbuf, outbuf,
    seg_stage, seg_x, seg_all,
    q_unit, k_unit, q_inv, k_inv, q_t, c_t, q_n, c_n, k_n, k_t, v_t, seg_col, seg_row,
    key_acc, value_acc, gain_acc, gain_send, gain_recv,
    load_sem, xs, xr, xsegs, xsegr, zs, zr, segs, segr, outs, outr, gs, gr,
):
    dp, z = lax.axis_index("dp"), lax.axis_index("seq")
    length = nz * ROWS
    lanes = nz * LANES
    partner = lax.rem(dp + ndp // 2, ndp)

    def remote(src, dst, send, recv, device):
        return pltpu.make_async_remote_copy(
            src_ref=src, dst_ref=dst, send_sem=send, recv_sem=recv,
            device_id=device, device_id_type=MESH,
        )

    def arrived(ref, sem):
        pltpu.make_async_copy(ref, ref, sem).wait()

    pairs = [(ref, raw.at[a]) for a, ref in enumerate((q_ref, k_ref, v_ref, c_ref))]
    pairs += [(seg_hbm, seg_ref), (qg_hbm, qg_ref), (kg_hbm, kg_ref)]
    loads = [
        pltpu.make_async_copy(src, dst, load_sem.at[i]) for i, (src, dst) in enumerate(pairs)
    ]
    for load in loads:
        load.start()

    by_distance = sorted(range(1, nz), key=lambda d: (-min(d, nz - d), d))

    bits = [1 << i for i in range(ndp.bit_length() - 1)]
    across = [dp + bit * (1 - 2 * lax.rem(dp // bit, 2)) for bit in bits]
    barrier = pltpu.get_barrier_semaphore()
    for peer in [(dp, lax.rem(z + d, nz)) for d in by_distance] + [(g, z) for g in across]:
        pl.semaphore_signal(barrier, inc=1, device_id=peer, device_id_type=MESH)

    def send_rows(p, slot, arrays):
        for d in by_distance:
            peer = lax.rem(z + d, nz)
            remote(
                stage.at[slot, arrays, :, pl.ds(pl.multiple_of(peer * LANES, LANES), LANES)],
                inbuf.at[p, arrays, pl.ds(pl.multiple_of(z * ROWS, ROWS), ROWS), :],
                zs.at[p], zr.at[p], (dp, peer),
            ).start()
        pltpu.make_async_copy(
            stage.at[slot, arrays, :, pl.ds(pl.multiple_of(z * LANES, LANES), LANES)],
            inbuf.at[p, arrays, pl.ds(pl.multiple_of(z * ROWS, ROWS), ROWS), :],
            zr.at[p],
        ).start()

    def send_ids(p, slot):
        seg_all[p, z] = seg_stage[slot]
        for d in by_distance:
            remote(
                seg_stage.at[slot], seg_all.at[p, z], segs.at[p], segr.at[p],
                (dp, lax.rem(z + d, nz)),
            ).start()

    def send_results(p):
        def put(peer, arrays):
            remote(
                outbuf.at[p, arrays, pl.ds(pl.multiple_of(peer * ROWS, ROWS), ROWS), :],
                ab_ref.at[p, arrays, :, pl.ds(pl.multiple_of(z * LANES, LANES), LANES)],
                outs.at[p], outr.at[p], (dp, peer),
            ).start()

        for d in by_distance:
            put(lax.rem(z + d, nz), pl.ds(0, 3))
        for j in range(nz - 1):
            put(j + jnp.where(j >= z, 1, 0), pl.ds(3, 1))
        pltpu.make_async_copy(
            outbuf.at[p, :, pl.ds(pl.multiple_of(z * ROWS, ROWS), ROWS), :],
            ab_ref.at[p, :, :, pl.ds(pl.multiple_of(z * LANES, LANES), LANES)],
            outr.at[p],
        ).start()

    moved = moved_ref[0]
    b_first = moved == 0
    pl.semaphore_wait(barrier, nz - 1 + len(bits))
    for a in range(4):
        loads[a].wait()
        stage[0, a] = jnp.where(b_first, raw[a, 1], raw[a, 0])
        send_rows(0, 0, pl.ds(a, 1))
    trades = []
    for a in range(4):
        stage[1, a] = jnp.where(b_first, raw[a, 0], raw[a, 1])
        trade = remote(stage.at[1, a], xrecv.at[a], xs.at[a], xr.at[a], (partner, z))
        trade.start()
        trades.append(trade)
    for load in loads[4:]:
        load.wait()
    segs_in = seg_ref[...].astype(F32)
    seg0 = jnp.broadcast_to(segs_in[0:1, 0:1], (8, LANES))
    seg1 = jnp.broadcast_to(segs_in[1:2, 0:1], (8, LANES))
    seg_stage[0] = jnp.where(b_first, seg1, seg0)
    seg_stage[1] = jnp.where(b_first, seg0, seg1)
    seg_trade = remote(seg_stage.at[1], seg_x, xsegs, xsegr, (partner, z))
    seg_trade.start()
    send_ids(0, 0)

    stays = moved == 2
    seg_trade.wait()
    seg_stage[2] = jnp.where(stays, seg_stage[1], seg_x[...])
    for a in range(4):
        trades[a].wait()
        stage[2, a] = jnp.where(stays, stage[1, a], xrecv[a])
    send_rows(1, 2, pl.ds(0, 4))
    send_ids(1, 2)

    q_gain, k_gain = column(qg_ref[...]), column(kg_ref[...])
    gain_acc[...] = jnp.zeros_like(gain_acc)

    def compute(p):
        top = lax.broadcasted_iota(jnp.int32, (LANES, length), 0) < HEAD_DIM
        left = lax.broadcasted_iota(jnp.int32, (length, LANES), 1) < HEAD_DIM

        def split_down(x):
            return jnp.where(top, x, 0.0).astype(BF16), jnp.where(top, 0.0, x).astype(BF16)

        def split_across(x):
            return jnp.where(left, x, 0.0).astype(BF16), jnp.where(left, 0.0, x).astype(BF16)

        ids = seg_all[p, :, 0:1, :]
        spread = jnp.broadcast_to(ids, (nz, ROWS, LANES)).reshape(length, LANES)
        seg_col[...] = spread
        seg_row[...] = jnp.transpose(spread)[0:8, :]

        unit, inv = normalize(jnp.transpose(inbuf[p, 0].astype(F32)))
        q_unit[...], q_inv[...] = unit, inv
        low = (unit * q_gain).astype(BF16).astype(F32) * SCALE
        q_t[0], q_t[1] = split_down(low)
        q_n[0], q_n[1] = split_across(jnp.transpose(low))

        unit, inv = normalize(jnp.transpose(inbuf[p, 1].astype(F32)))
        k_unit[...], k_inv[...] = unit, inv
        low = (unit * k_gain).astype(BF16).astype(F32)
        k_t[...] = low.astype(BF16)
        k_n[...] = jnp.transpose(low).astype(BF16)

        v_t[...] = jnp.transpose(inbuf[p, 2].astype(F32)).astype(BF16)
        cot = inbuf[p, 3].astype(F32)
        c_n[0], c_n[1] = split_across(cot)
        c_t[0], c_t[1] = split_down(jnp.transpose(cot))
        key_acc[...] = jnp.zeros_like(key_acc)
        value_acc[...] = jnp.zeros_like(value_acc)

        def step(i, carry):
            at = pl.ds(pl.multiple_of(i * block, block), block)
            wide = jnp.concatenate([seg_col[...]] * (block // LANES), axis=1)
            same = wide == seg_row[0:1, at]
            attended, grad = [], []
            for h in range(2):
                head = pl.ds(h * HEAD_DIM, HEAD_DIM)
                scores = jnp.where(same, dot(k_n[...], q_t[h, :, at]), MASKED)
                exponent = jnp.exp(scores - jnp.max(scores, axis=0, keepdims=True))
                weights = exponent * (1.0 / jnp.sum(exponent, axis=0, keepdims=True))
                weights_low = weights.astype(BF16)
                full = dot(v_t[head, :], weights_low)
                delta = jnp.sum(c_t[h, head, at].astype(F32) * full, axis=0, keepdims=True)
                prob_grad = dot(inbuf[p, 2], c_t[h, :, at])
                score_grad = (weights * (prob_grad - delta)).astype(BF16)
                value_acc[...] += dot(weights_low, c_n[h, at, :])
                key_acc[...] += dot(score_grad, q_n[h, at, :])
                attended.append(full)
                grad.append(dot(k_t[head, :], score_grad) * SCALE)
            outbuf[p, 0, at, :] = jnp.transpose(jnp.concatenate(attended, axis=0)).astype(BF16)
            grad = jnp.concatenate(grad, axis=0)
            unit = q_unit[:, at]
            gain_acc[0] += fold_lanes(grad * unit)
            back = norm_back(grad, unit, q_inv[:, :, at], q_gain)
            outbuf[p, 1, at, :] = jnp.transpose(back).astype(BF16)
            return carry

        lax.fori_loop(0, length // block, step, 0)
        outbuf[p, 3] = value_acc[...].astype(BF16)
        grad = jnp.transpose(key_acc[...])
        unit = k_unit[...]
        gain_acc[1] += fold_lanes(grad * unit)
        back = norm_back(grad, unit, k_inv[...], k_gain)
        outbuf[p, 2] = jnp.transpose(back).astype(BF16)

    for p in range(2):
        arrived(inbuf.at[p], zr.at[p])
        arrived(seg_all.at[p, pl.ds(0, nz - 1)], segr.at[p])
        compute(p)
        send_results(p)

    rows = [jnp.sum(jnp.transpose(gain_acc[i]), axis=0, keepdims=True) for i in range(2)]
    pick = lax.broadcasted_iota(jnp.int32, (8, LANES), 0)
    total = jnp.where(pick == 0, rows[0], jnp.where(pick == 1, rows[1], 0.0))
    for i, group in enumerate(across):
        gain_send[i] = total
        swap = remote(gain_send.at[i], gain_recv.at[i], gs.at[i], gr.at[i], (group, z))
        swap.start()
        swap.wait()
        total = total + gain_recv[i]
    gain_ref[...] = total

    for p in range(2):
        arrived(ab_ref.at[p], outr.at[p])
        arrived(stage.at[2 * p, :, :, pl.ds(0, lanes - LANES)], zs.at[p])
        arrived(seg_all.at[p, pl.ds(0, nz - 1)], segs.at[p])
        arrived(outbuf.at[p, :, pl.ds(0, length - ROWS), :], outs.at[p])


def place_kernel(
    moved_ref, ab_ref, gain_ref, out0, out1, out2, out3, gq_ref, gk_ref, held, in_sem, out_sem
):
    dp = lax.axis_index("dp")
    b_slot = jnp.where(moved_ref[0] == 0, 0, 1)
    pairs = [(a, p) for p in range(2) for a in range(4)]
    outs = (out0, out1, out2, out3)
    loads = [
        pltpu.make_async_copy(ab_ref.at[p, a], held.at[p, a], in_sem.at[p, a]) for a, p in pairs
    ]
    stores = [
        pltpu.make_async_copy(
            held.at[p, a], outs[a].at[1 - b_slot if p == 0 else b_slot], out_sem.at[p, a]
        )
        for a, p in pairs
    ]
    for load in loads:
        load.start()
    for load, store in zip(loads, stores):
        load.wait()
        store.start()
    lane = lax.broadcasted_iota(jnp.int32, (1, LANES), 1)
    down = lax.broadcasted_iota(jnp.int32, (2, 2), 0)
    across = lax.broadcasted_iota(jnp.int32, (2, 2), 1)
    for i, ref in enumerate((gq_ref, gk_ref)):
        row = gain_ref[i : i + 1, :]
        total = jnp.zeros((2, 2), F32)
        for h in range(2):
            for j in range(2):
                chosen = lane == h * HEAD_DIM + 2 * dp + j
                value = jnp.sum(jnp.where(chosen, row, 0.0), axis=1, keepdims=True)
                total = jnp.where((down == h) & (across == j), value, total)
        ref[...] = total
    for store in stores:
        store.wait()


def body(nz, ndp, q, k, v, c, seg, moved, q_gain, k_gain):
    length, lanes = nz * ROWS, nz * LANES
    block = min(256, length)
    hops = ndp.bit_length() - 1
    anywhere = pl.BlockSpec(memory_space=pl.ANY)
    vmem = pl.BlockSpec(memory_space=pltpu.VMEM)
    smem = pl.BlockSpec(memory_space=pltpu.SMEM)
    dma = pltpu.SemaphoreType.DMA
    ab, gains = pl.pallas_call(
        functools.partial(main_kernel, nz, ndp, block),
        out_shape=(
            jax.ShapeDtypeStruct((2, 4, ROWS, lanes), BF16),
            jax.ShapeDtypeStruct((8, LANES), F32),
        ),
        in_specs=[smem] + [pl.BlockSpec(memory_space=pltpu.HBM)] * 7,
        out_specs=(anywhere, vmem),
        scratch_shapes=[
            pltpu.VMEM((4, 2, ROWS, lanes), BF16),
            pltpu.VMEM((2, ROWS), jnp.int32),
            pltpu.VMEM((2, HEAD_DIM), F32),
            pltpu.VMEM((2, HEAD_DIM), F32),
            pltpu.VMEM((3, 4, ROWS, lanes), BF16),
            pltpu.VMEM((4, ROWS, lanes), BF16),
            pltpu.VMEM((2, 4, length, LANES), BF16),
            pltpu.VMEM((2, 4, length, LANES), BF16),
            pltpu.VMEM((3, 8, LANES), F32),
            pltpu.VMEM((8, LANES), F32),
            pltpu.VMEM((2, nz, 8, LANES), F32),
            pltpu.VMEM((LANES, length), F32),
            pltpu.VMEM((LANES, length), F32),
            pltpu.VMEM((2, 1, length), F32),
            pltpu.VMEM((2, 1, length), F32),
            pltpu.VMEM((2, LANES, length), BF16),
            pltpu.VMEM((2, LANES, length), BF16),
            pltpu.VMEM((2, length, LANES), BF16),
            pltpu.VMEM((2, length, LANES), BF16),
            pltpu.VMEM((length, LANES), BF16),
            pltpu.VMEM((LANES, length), BF16),
            pltpu.VMEM((LANES, length), BF16),
            pltpu.VMEM((length, LANES), F32),
            pltpu.VMEM((8, length), F32),
            pltpu.VMEM((length, LANES), F32),
            pltpu.VMEM((length, LANES), F32),
            pltpu.VMEM((2, LANES, LANES), F32),
            pltpu.VMEM((hops, 8, LANES), F32),
            pltpu.VMEM((hops, 8, LANES), F32),
            dma((7,)),
            dma((4,)), dma((4,)), dma(()), dma(()),
            dma((2,)), dma((2,)), dma((2,)), dma((2,)),
            dma((2,)), dma((2,)), dma((hops,)), dma((hops,)),
        ],
        compiler_params=pltpu.CompilerParams(
            collective_id=0, has_side_effects=True, vmem_limit_bytes=60 << 20
        ),
        name="attend",
    )(moved, q, k, v, c, seg, q_gain, k_gain)
    rows = jax.ShapeDtypeStruct((2, ROWS, lanes), BF16)
    small = jax.ShapeDtypeStruct((2, 2), F32)
    return pl.pallas_call(
        place_kernel,
        out_shape=(rows, rows, rows, rows, small, small),
        in_specs=[smem, anywhere, vmem],
        out_specs=(anywhere,) * 4 + (vmem, vmem),
        scratch_shapes=[pltpu.VMEM((2, 4, ROWS, lanes), BF16), dma((2, 4)), dma((2, 4))],
        compiler_params=pltpu.CompilerParams(vmem_limit_bytes=60 << 20),
        name="place",
    )(moved, ab, gains)


def solution(mesh):
    return jax.shard_map(
        functools.partial(body, mesh.shape["seq"], mesh.shape["dp"]),
        mesh=mesh,
        in_specs=(
            P("dp", "seq", None),
            P("dp", "seq", None),
            P("dp", "seq", None),
            P("dp", "seq", None),
            P("dp", "seq"),
            P("dp"),
            P("seq", None),
            P("seq", None),
        ),
        out_specs=(
            P("dp", "seq", None),
            P("dp", "seq", None),
            P("dp", "seq", None),
            P("dp", "seq", None),
            P("seq", "dp"),
            P("seq", "dp"),
        ),
        check_vma=False,
    )
```

```python
import functools

import jax
import jax.numpy as jnp
from jax import lax
from jax.experimental import pallas as pl
from jax.experimental.pallas import tpu as pltpu
from jax.sharding import PartitionSpec as P

MESH = pl.DeviceIdType.MESH
HEAD_DIM = 64
EPSILON = 1e-06
ROWS = 64
LANES = 128
SCALE = HEAD_DIM ** (-0.5)
MASKED = -1e30
F32 = jnp.float32
BF16 = jnp.bfloat16


def dot(a, b):
    return jnp.dot(a, b, preferred_element_type=F32)


def column(gain):
    row = jnp.concatenate([gain[0:1, :], gain[1:2, :]], axis=1)
    return jnp.transpose(jnp.broadcast_to(row, (LANES, LANES)))[:, 0:1]


def normalize(raw):
    parts = raw.reshape(2, HEAD_DIM, raw.shape[1])
    centred = parts - jnp.mean(parts, axis=1, keepdims=True)
    inv_std = lax.rsqrt(jnp.mean(centred * centred, axis=1, keepdims=True) + EPSILON)
    return (centred * inv_std).reshape(raw.shape), inv_std


def norm_back(grad, unit_rows, inv_std, gain):
    scaled = (grad * gain).reshape(2, HEAD_DIM, grad.shape[1])
    unit = unit_rows.reshape(scaled.shape)
    inner = (
        scaled
        - jnp.mean(scaled, axis=1, keepdims=True)
        - unit * jnp.mean(scaled * unit, axis=1, keepdims=True)
    )
    return (inv_std * inner).reshape(grad.shape)


def fold_lanes(x):
    total = x[:, 0:LANES]
    for start in range(LANES, x.shape[1], LANES):
        total = total + x[:, start : start + LANES]
    return total


def main_kernel(
    nz, ndp, block,
    moved_hbm, q_ref, k_ref, v_ref, c_ref, seg_hbm, qg_hbm, kg_hbm,
    ab_ref, gain_ref,
    raw, moved_ref, seg_ref, qg_ref, kg_ref, stage, xrecv, inbuf, outbuf,
    seg_stage, seg_x, seg_all,
    q_unit, k_unit, q_inv, k_inv, q_t, c_t, q_n, c_n, k_n, k_t, v_t, seg_col, seg_row,
    key_acc, value_acc, gain_acc, gain_send, gain_recv, gain_sum,
    known, load_sem, xs, xr, xsegs, xsegr, zs, zr, segs, segr, outs, outr, gs, gr,
):
    dp, z = lax.axis_index("dp"), lax.axis_index("seq")
    length = nz * ROWS
    lanes = nz * LANES
    partner = lax.rem(dp + ndp // 2, ndp)

    def remote(src, dst, send, recv, device):
        return pltpu.make_async_remote_copy(
            src_ref=src, dst_ref=dst, send_sem=send, recv_sem=recv,
            device_id=device, device_id_type=MESH,
        )

    def arrived(ref, sem):
        pltpu.make_async_copy(ref, ref, sem).wait()

    pairs = [(ref, raw.at[a]) for a, ref in enumerate((q_ref, k_ref, v_ref, c_ref))]
    pairs += [(seg_hbm, seg_ref), (qg_hbm, qg_ref), (kg_hbm, kg_ref), (moved_hbm, moved_ref)]
    loads = [
        pltpu.make_async_copy(src, dst, load_sem.at[i]) for i, (src, dst) in enumerate(pairs)
    ]
    for load in [loads[-1]] + loads[:-1]:
        load.start()

    by_distance = sorted(range(1, nz), key=lambda d: (-min(d, nz - d), d))

    bits = [1 << i for i in range(ndp.bit_length() - 1)]
    across = [dp + bit * (1 - 2 * lax.rem(dp // bit, 2)) for bit in bits]
    beside = [(dp, lax.rem(z + 1, nz)), (dp, lax.rem(z + nz - 1, nz))]
    barrier = pltpu.get_barrier_semaphore()
    for peer in beside + [(g, z) for g in across]:
        pl.semaphore_signal(barrier, inc=1, device_id=peer, device_id_type=MESH)

    def tell(k):
        for peer in beside:
            pl.semaphore_signal(known.at[k - 1], inc=1, device_id=peer, device_id_type=MESH)

    def pair(k):
        return [k, nz - k] if k < nz - k else [k]

    def send_rows(p, slot, arrays, distances):
        for d in distances:
            peer = lax.rem(z + d, nz)
            remote(
                stage.at[slot, arrays, :, pl.ds(pl.multiple_of(peer * LANES, LANES), LANES)],
                inbuf.at[p, arrays, pl.ds(pl.multiple_of(z * ROWS, ROWS), ROWS), :],
                zs.at[p], zr.at[p], (dp, peer),
            ).start()

    def keep_rows(p, slot):
        pltpu.make_async_copy(
            stage.at[slot, :, :, pl.ds(pl.multiple_of(z * LANES, LANES), LANES)],
            inbuf.at[p, :, pl.ds(pl.multiple_of(z * ROWS, ROWS), ROWS), :],
            zr.at[p],
        ).start()

    def send_ids(p, slot):
        seg_all[p, z] = seg_stage[slot]
        for d in by_distance:
            remote(
                seg_stage.at[slot], seg_all.at[p, z], segs.at[p], segr.at[p],
                (dp, lax.rem(z + d, nz)),
            ).start()

    def send_results(p):
        def put(peer):
            remote(
                outbuf.at[p, :, pl.ds(pl.multiple_of(peer * ROWS, ROWS), ROWS), :],
                ab_ref.at[p, :, :, pl.ds(pl.multiple_of(z * LANES, LANES), LANES)],
                outs.at[p], outr.at[p], (dp, peer),
            ).start()

        first = nz * 7 // 16
        for peer in range(first):

            @pl.when(z != peer)
            def _():
                put(peer)

        for d in by_distance:
            peer = lax.rem(z + d, nz)

            @pl.when(peer >= first)
            def _():
                put(peer)

        pltpu.make_async_copy(
            outbuf.at[p, :, pl.ds(pl.multiple_of(z * ROWS, ROWS), ROWS), :],
            ab_ref.at[p, :, :, pl.ds(pl.multiple_of(z * LANES, LANES), LANES)],
            outr.at[p],
        ).start()

    loads[-1].wait()
    moved = moved_ref[0]
    b_first = moved == 0
    pl.semaphore_wait(barrier, 2 + len(bits))
    far = nz // 2
    if far > 1:
        tell(1)
    for a in range(4):
        loads[a].wait()
        stage[0, a] = jnp.where(b_first, raw[a, 1], raw[a, 0])
        send_rows(0, 0, pl.ds(a, 1), pair(1))
    for k in range(2, far + 1):
        pl.semaphore_wait(known.at[k - 2], 2)
        if k < far:
            tell(k)
        send_rows(0, 0, pl.ds(0, 4), pair(k))
    keep_rows(0, 0)
    trades = []
    for a in range(4):
        stage[1, a] = jnp.where(b_first, raw[a, 0], raw[a, 1])
        trade = remote(stage.at[1, a], xrecv.at[a], xs.at[a], xr.at[a], (partner, z))
        trade.start()
        trades.append(trade)
    for load in loads[4:-1]:
        load.wait()
    segs_in = seg_ref[...].astype(F32)
    seg0 = jnp.broadcast_to(segs_in[0:1, 0:1], (8, LANES))
    seg1 = jnp.broadcast_to(segs_in[1:2, 0:1], (8, LANES))
    seg_stage[0] = jnp.where(b_first, seg1, seg0)
    seg_stage[1] = jnp.where(b_first, seg0, seg1)
    seg_trade = remote(seg_stage.at[1], seg_x, xsegs, xsegr, (partner, z))
    seg_trade.start()
    send_ids(0, 0)

    stays = moved == 2
    seg_trade.wait()
    seg_stage[2] = jnp.where(stays, seg_stage[1], seg_x[...])
    for a in range(4):
        trades[a].wait()
        stage[2, a] = jnp.where(stays, stage[1, a], xrecv[a])
    send_rows(1, 2, pl.ds(0, 4), by_distance)
    keep_rows(1, 2)
    send_ids(1, 2)

    q_gain, k_gain = column(qg_ref[...]), column(kg_ref[...])
    gain_acc[...] = jnp.zeros_like(gain_acc)

    def compute(p):
        top = lax.broadcasted_iota(jnp.int32, (LANES, length), 0) < HEAD_DIM
        left = lax.broadcasted_iota(jnp.int32, (length, LANES), 1) < HEAD_DIM

        def split_down(x):
            return jnp.where(top, x, 0.0).astype(BF16), jnp.where(top, 0.0, x).astype(BF16)

        def split_across(x):
            return jnp.where(left, x, 0.0).astype(BF16), jnp.where(left, 0.0, x).astype(BF16)

        ids = seg_all[p, :, 0:1, :]
        spread = jnp.broadcast_to(ids, (nz, ROWS, LANES)).reshape(length, LANES)
        seg_col[...] = spread
        seg_row[...] = jnp.transpose(spread)[0:8, :]

        unit, inv = normalize(jnp.transpose(inbuf[p, 0].astype(F32)))
        q_unit[...], q_inv[...] = unit, inv
        low = (unit * q_gain).astype(BF16).astype(F32) * SCALE
        q_t[0], q_t[1] = split_down(low)
        q_n[0], q_n[1] = split_across(jnp.transpose(low))

        unit, inv = normalize(jnp.transpose(inbuf[p, 1].astype(F32)))
        k_unit[...], k_inv[...] = unit, inv
        low = (unit * k_gain).astype(BF16).astype(F32)
        k_t[...] = low.astype(BF16)
        k_n[...] = jnp.transpose(low).astype(BF16)

        v_t[...] = jnp.transpose(inbuf[p, 2].astype(F32)).astype(BF16)
        cot = inbuf[p, 3].astype(F32)
        c_n[0], c_n[1] = split_across(cot)
        c_t[0], c_t[1] = split_down(jnp.transpose(cot))
        key_acc[...] = jnp.zeros_like(key_acc)
        value_acc[...] = jnp.zeros_like(value_acc)

        def step(i, carry):
            at = pl.ds(pl.multiple_of(i * block, block), block)
            wide = jnp.concatenate([seg_col[...]] * (block // LANES), axis=1)
            same = wide == seg_row[0:1, at]
            attended, grad = [], []
            for h in range(2):
                head = pl.ds(h * HEAD_DIM, HEAD_DIM)
                scores = jnp.where(same, dot(k_n[...], q_t[h, :, at]), MASKED)
                exponent = jnp.exp(scores - jnp.max(scores, axis=0, keepdims=True))
                weights = exponent * (1.0 / jnp.sum(exponent, axis=0, keepdims=True))
                weights_low = weights.astype(BF16)
                full = dot(v_t[head, :], weights_low)
                delta = jnp.sum(c_t[h, head, at].astype(F32) * full, axis=0, keepdims=True)
                prob_grad = dot(inbuf[p, 2], c_t[h, :, at])
                score_grad = (weights * (prob_grad - delta)).astype(BF16)
                value_acc[...] += dot(weights_low, c_n[h, at, :])
                key_acc[...] += dot(score_grad, q_n[h, at, :])
                attended.append(full)
                grad.append(dot(k_t[head, :], score_grad) * SCALE)
            outbuf[p, 0, at, :] = jnp.transpose(jnp.concatenate(attended, axis=0)).astype(BF16)
            grad = jnp.concatenate(grad, axis=0)
            unit = q_unit[:, at]
            gain_acc[0] += fold_lanes(grad * unit)
            back = norm_back(grad, unit, q_inv[:, :, at], q_gain)
            outbuf[p, 1, at, :] = jnp.transpose(back).astype(BF16)
            return carry

        lax.fori_loop(0, length // block, step, 0)
        outbuf[p, 3] = value_acc[...].astype(BF16)
        grad = jnp.transpose(key_acc[...])
        unit = k_unit[...]
        gain_acc[1] += fold_lanes(grad * unit)
        back = norm_back(grad, unit, k_inv[...], k_gain)
        outbuf[p, 2] = jnp.transpose(back).astype(BF16)

    for p in range(2):
        arrived(inbuf.at[p], zr.at[p])
        arrived(seg_all.at[p, pl.ds(0, nz - 1)], segr.at[p])
        compute(p)
        send_results(p)

    rows = [jnp.sum(jnp.transpose(gain_acc[i]), axis=0, keepdims=True) for i in range(2)]
    pick = lax.broadcasted_iota(jnp.int32, (8, LANES), 0)
    total = jnp.where(pick == 0, rows[0], jnp.where(pick == 1, rows[1], 0.0))
    for i, group in enumerate(across):
        gain_send[i] = total
        swap = remote(gain_send.at[i], gain_recv.at[i], gs.at[i], gr.at[i], (group, z))
        swap.start()
        swap.wait()
        total = total + gain_recv[i]
    gain_sum[...] = total
    gain_out = pltpu.make_async_copy(gain_sum, gain_ref, load_sem.at[0])
    gain_out.start()

    for p in range(2):
        arrived(ab_ref.at[p], outr.at[p])
        arrived(stage.at[2 * p, :, :, pl.ds(0, lanes - LANES)], zs.at[p])
        arrived(seg_all.at[p, pl.ds(0, nz - 1)], segs.at[p])
        arrived(outbuf.at[p, :, pl.ds(0, length - ROWS), :], outs.at[p])
    gain_out.wait()


def place_kernel(
    moved_hbm, ab_ref, gain_hbm, out0, out1, out2, out3, gq_ref, gk_ref,
    held, moved_ref, gain_ref, gain_low, in_sem, out_sem, small_sem,
):
    moved_in = pltpu.make_async_copy(moved_hbm, moved_ref, small_sem.at[0])
    gain_in = pltpu.make_async_copy(gain_hbm, gain_ref, small_sem.at[1])
    moved_in.start()
    pairs = [(a, p) for p in range(2) for a in range(4)]
    loads = [
        pltpu.make_async_copy(ab_ref.at[p, a], held.at[p, a], in_sem.at[p, a]) for a, p in pairs
    ]
    for load in loads:
        load.start()
    gain_in.start()
    moved_in.wait()
    b_slot = jnp.where(moved_ref[0] == 0, 0, 1)
    outs = (out0, out1, out2, out3)
    stores = []
    for load, (a, p) in zip(loads, pairs):
        slot = 1 - b_slot if p == 0 else b_slot
        load.wait()
        stores.append(
            pltpu.make_async_copy(held.at[p, a], outs[a].at[slot], out_sem.at[p, a])
        )
        stores[-1].start()
    gain_in.wait()
    dp = lax.axis_index("dp")
    lane = lax.broadcasted_iota(jnp.int32, (1, LANES), 1)
    down = lax.broadcasted_iota(jnp.int32, (2, 2), 0)
    across = lax.broadcasted_iota(jnp.int32, (2, 2), 1)
    for i, ref in enumerate((gq_ref, gk_ref)):
        row = gain_ref[i : i + 1, :]
        total = jnp.zeros((2, 2), F32)
        for h in range(2):
            for j in range(2):
                chosen = lane == h * HEAD_DIM + 2 * dp + j
                value = jnp.sum(jnp.where(chosen, row, 0.0), axis=1, keepdims=True)
                total = jnp.where((down == h) & (across == j), value, total)
        gain_low[i] = total
        stores.append(pltpu.make_async_copy(gain_low.at[i], ref, small_sem.at[2 + i]))
        stores[-1].start()
    for store in stores:
        store.wait()


def body(nz, ndp, q, k, v, c, seg, moved, q_gain, k_gain):
    length, lanes = nz * ROWS, nz * LANES
    block = min(256, length)
    hops = ndp.bit_length() - 1
    anywhere = pl.BlockSpec(memory_space=pl.ANY)
    dma = pltpu.SemaphoreType.DMA
    ab, gains = pl.pallas_call(
        functools.partial(main_kernel, nz, ndp, block),
        out_shape=(
            jax.ShapeDtypeStruct((2, 4, ROWS, lanes), BF16),
            jax.ShapeDtypeStruct((8, LANES), F32),
        ),
        in_specs=[anywhere] * 8,
        out_specs=(anywhere, anywhere),
        scratch_shapes=[
            pltpu.VMEM((4, 2, ROWS, lanes), BF16),
            pltpu.SMEM((1,), jnp.int32),
            pltpu.VMEM((2, ROWS), jnp.int32),
            pltpu.VMEM((2, HEAD_DIM), F32),
            pltpu.VMEM((2, HEAD_DIM), F32),
            pltpu.VMEM((3, 4, ROWS, lanes), BF16),
            pltpu.VMEM((4, ROWS, lanes), BF16),
            pltpu.VMEM((2, 4, length, LANES), BF16),
            pltpu.VMEM((2, 4, length, LANES), BF16),
            pltpu.VMEM((3, 8, LANES), F32),
            pltpu.VMEM((8, LANES), F32),
            pltpu.VMEM((2, nz, 8, LANES), F32),
            pltpu.VMEM((LANES, length), F32),
            pltpu.VMEM((LANES, length), F32),
            pltpu.VMEM((2, 1, length), F32),
            pltpu.VMEM((2, 1, length), F32),
            pltpu.VMEM((2, LANES, length), BF16),
            pltpu.VMEM((2, LANES, length), BF16),
            pltpu.VMEM((2, length, LANES), BF16),
            pltpu.VMEM((2, length, LANES), BF16),
            pltpu.VMEM((length, LANES), BF16),
            pltpu.VMEM((LANES, length), BF16),
            pltpu.VMEM((LANES, length), BF16),
            pltpu.VMEM((length, LANES), F32),
            pltpu.VMEM((8, length), F32),
            pltpu.VMEM((length, LANES), F32),
            pltpu.VMEM((length, LANES), F32),
            pltpu.VMEM((2, LANES, LANES), F32),
            pltpu.VMEM((hops, 8, LANES), F32),
            pltpu.VMEM((hops, 8, LANES), F32),
            pltpu.VMEM((8, LANES), F32),
            pltpu.SemaphoreType.REGULAR((max(1, nz // 2 - 1),)),
            dma((8,)),
            dma((4,)), dma((4,)), dma(()), dma(()),
            dma((2,)), dma((2,)), dma((2,)), dma((2,)),
            dma((2,)), dma((2,)), dma((hops,)), dma((hops,)),
        ],
        compiler_params=pltpu.CompilerParams(
            collective_id=0, has_side_effects=True, vmem_limit_bytes=60 << 20
        ),
        name="attend",
    )(moved, q, k, v, c, seg, q_gain, k_gain)
    rows = jax.ShapeDtypeStruct((2, ROWS, lanes), BF16)
    small = jax.ShapeDtypeStruct((2, 2), F32)
    return pl.pallas_call(
        place_kernel,
        out_shape=(rows, rows, rows, rows, small, small),
        in_specs=[anywhere] * 3,
        out_specs=(anywhere,) * 6,
        scratch_shapes=[
            pltpu.VMEM((2, 4, ROWS, lanes), BF16),
            pltpu.SMEM((1,), jnp.int32),
            pltpu.VMEM((8, LANES), F32),
            pltpu.VMEM((2, 2, 2), F32),
            dma((2, 4)), dma((2, 4)), dma((4,)),
        ],
        compiler_params=pltpu.CompilerParams(vmem_limit_bytes=60 << 20),
        name="place",
    )(moved, ab, gains)


def solution(mesh):
    return jax.shard_map(
        functools.partial(body, mesh.shape["seq"], mesh.shape["dp"]),
        mesh=mesh,
        in_specs=(
            P("dp", "seq", None),
            P("dp", "seq", None),
            P("dp", "seq", None),
            P("dp", "seq", None),
            P("dp", "seq"),
            P("dp"),
            P("seq", None),
            P("seq", None),
        ),
        out_specs=(
            P("dp", "seq", None),
            P("dp", "seq", None),
            P("dp", "seq", None),
            P("dp", "seq", None),
            P("seq", "dp"),
            P("seq", "dp"),
        ),
        check_vma=False,
    )
```

```python
import functools

import jax
import jax.numpy as jnp
from jax import lax
from jax.experimental import pallas as pl
from jax.experimental.pallas import tpu as pltpu
from jax.sharding import PartitionSpec as P

MESH = pl.DeviceIdType.MESH
HEAD_DIM = 64
EPSILON = 1e-06
ROWS = 64
LANES = 128
SCALE = HEAD_DIM ** (-0.5)
MASKED = -1e30
F32 = jnp.float32
BF16 = jnp.bfloat16


def dot(a, b):
    return jnp.dot(a, b, preferred_element_type=F32)


def column(gain):
    row = jnp.concatenate([gain[0:1, :], gain[1:2, :]], axis=1)
    return jnp.transpose(jnp.broadcast_to(row, (LANES, LANES)))[:, 0:1]


def normalize(raw):
    parts = raw.reshape(2, HEAD_DIM, raw.shape[1])
    centred = parts - jnp.mean(parts, axis=1, keepdims=True)
    inv_std = lax.rsqrt(jnp.mean(centred * centred, axis=1, keepdims=True) + EPSILON)
    return (centred * inv_std).reshape(raw.shape), inv_std


def norm_back(grad, unit_rows, inv_std, gain):
    scaled = (grad * gain).reshape(2, HEAD_DIM, grad.shape[1])
    unit = unit_rows.reshape(scaled.shape)
    inner = (
        scaled
        - jnp.mean(scaled, axis=1, keepdims=True)
        - unit * jnp.mean(scaled * unit, axis=1, keepdims=True)
    )
    return (inv_std * inner).reshape(grad.shape)


def fold_lanes(x):
    total = x[:, 0:LANES]
    for start in range(LANES, x.shape[1], LANES):
        total = total + x[:, start : start + LANES]
    return total


def main_kernel(
    nz, ndp, block,
    moved_hbm, q_ref, k_ref, v_ref, c_ref, seg_hbm, qg_hbm, kg_hbm,
    ab_ref, gain_ref,
    raw, moved_ref, seg_ref, qg_ref, kg_ref, stage, xrecv, inbuf, outbuf,
    seg_stage, seg_x, seg_all,
    q_unit, k_unit, q_inv, k_inv, q_t, c_t, q_n, c_n, k_n, k_t, v_t, seg_col, seg_row,
    key_acc, value_acc, gain_acc, gain_send, gain_recv, gain_sum,
    known, load_sem, xs, xr, xsegs, xsegr, zs, zr, segs, segr, outs, outr, gs, gr,
):
    dp, z = lax.axis_index("dp"), lax.axis_index("seq")
    length = nz * ROWS
    lanes = nz * LANES
    partner = lax.rem(dp + ndp // 2, ndp)

    def remote(src, dst, send, recv, device):
        return pltpu.make_async_remote_copy(
            src_ref=src, dst_ref=dst, send_sem=send, recv_sem=recv,
            device_id=device, device_id_type=MESH,
        )

    def arrived(ref, sem):
        pltpu.make_async_copy(ref, ref, sem).wait()

    pairs = [(ref, raw.at[a]) for a, ref in enumerate((q_ref, k_ref, v_ref, c_ref))]
    pairs += [(seg_hbm, seg_ref), (qg_hbm, qg_ref), (kg_hbm, kg_ref), (moved_hbm, moved_ref)]
    loads = [
        pltpu.make_async_copy(src, dst, load_sem.at[i]) for i, (src, dst) in enumerate(pairs)
    ]
    for load in [loads[-1]] + loads[:-1]:
        load.start()

    by_distance = sorted(range(1, nz), key=lambda d: (-min(d, nz - d), d))

    bits = [1 << i for i in range(ndp.bit_length() - 1)]
    across = [dp + bit * (1 - 2 * lax.rem(dp // bit, 2)) for bit in bits]
    beside = [(dp, lax.rem(z + 1, nz)), (dp, lax.rem(z + nz - 1, nz))]
    barrier = pltpu.get_barrier_semaphore()
    for peer in beside + [(g, z) for g in across]:
        pl.semaphore_signal(barrier, inc=1, device_id=peer, device_id_type=MESH)

    def tell(k):
        for peer in beside:
            pl.semaphore_signal(known.at[k - 1], inc=1, device_id=peer, device_id_type=MESH)

    def pair(k):
        return [k, nz - k] if k < nz - k else [k]

    def send_rows(p, slot, arrays, distances):
        for d in distances:
            peer = lax.rem(z + d, nz)
            remote(
                stage.at[slot, arrays, :, pl.ds(pl.multiple_of(peer * LANES, LANES), LANES)],
                inbuf.at[p, arrays, pl.ds(pl.multiple_of(z * ROWS, ROWS), ROWS), :],
                zs.at[p], zr.at[p], (dp, peer),
            ).start()

    def keep_rows(p, slot):
        pltpu.make_async_copy(
            stage.at[slot, :, :, pl.ds(pl.multiple_of(z * LANES, LANES), LANES)],
            inbuf.at[p, :, pl.ds(pl.multiple_of(z * ROWS, ROWS), ROWS), :],
            zr.at[p],
        ).start()

    def send_ids(p, slot):
        seg_all[p, z] = seg_stage[slot]
        for d in by_distance:
            remote(
                seg_stage.at[slot], seg_all.at[p, z], segs.at[p], segr.at[p],
                (dp, lax.rem(z + d, nz)),
            ).start()

    def send_results(p):
        def put(peer):
            remote(
                outbuf.at[p, :, pl.ds(pl.multiple_of(peer * ROWS, ROWS), ROWS), :],
                ab_ref.at[p, :, :, pl.ds(pl.multiple_of(z * LANES, LANES), LANES)],
                outs.at[p], outr.at[p], (dp, peer),
            ).start()

        first = nz * 7 // 16
        for peer in range(first):

            @pl.when(z != peer)
            def _():
                put(peer)

        for d in by_distance:
            peer = lax.rem(z + d, nz)

            @pl.when(peer >= first)
            def _():
                put(peer)

        pltpu.make_async_copy(
            outbuf.at[p, :, pl.ds(pl.multiple_of(z * ROWS, ROWS), ROWS), :],
            ab_ref.at[p, :, :, pl.ds(pl.multiple_of(z * LANES, LANES), LANES)],
            outr.at[p],
        ).start()

    loads[-1].wait()
    moved = moved_ref[0]
    b_first = moved == 0
    pl.semaphore_wait(barrier, 2 + len(bits))
    far = nz // 2
    if far > 1:
        tell(1)
    for a in range(4):
        loads[a].wait()
        stage[0, a] = jnp.where(b_first, raw[a, 1], raw[a, 0])
        send_rows(0, 0, pl.ds(a, 1), pair(1))
    for k in range(2, far + 1):
        pl.semaphore_wait(known.at[k - 2], 2)
        if k < far:
            tell(k)
        send_rows(0, 0, pl.ds(0, 4), pair(k))
    keep_rows(0, 0)
    trades = []
    for a in range(4):
        stage[1, a] = jnp.where(b_first, raw[a, 0], raw[a, 1])
        trade = remote(stage.at[1, a], xrecv.at[a], xs.at[a], xr.at[a], (partner, z))
        trade.start()
        trades.append(trade)
    for load in loads[4:-1]:
        load.wait()
    segs_in = seg_ref[...].astype(F32)
    seg0 = jnp.broadcast_to(segs_in[0:1, 0:1], (1, LANES))
    seg1 = jnp.broadcast_to(segs_in[1:2, 0:1], (1, LANES))
    seg_stage[0] = jnp.where(b_first, seg1, seg0)
    seg_stage[1] = jnp.where(b_first, seg0, seg1)
    seg_trade = remote(seg_stage.at[1], seg_x, xsegs, xsegr, (partner, z))
    seg_trade.start()
    send_ids(0, 0)

    stays = moved == 2
    seg_trade.wait()
    seg_stage[2] = jnp.where(stays, seg_stage[1], seg_x[...])
    for a in range(4):
        trades[a].wait()
        stage[2, a] = jnp.where(stays, stage[1, a], xrecv[a])
    send_rows(1, 2, pl.ds(0, 4), by_distance)
    keep_rows(1, 2)
    send_ids(1, 2)

    q_gain, k_gain = column(qg_ref[...]), column(kg_ref[...])
    gain_acc[...] = jnp.zeros_like(gain_acc)

    def compute(p):
        top = lax.broadcasted_iota(jnp.int32, (LANES, length), 0) < HEAD_DIM
        left = lax.broadcasted_iota(jnp.int32, (length, LANES), 1) < HEAD_DIM

        def split_down(x):
            return jnp.where(top, x, 0.0).astype(BF16), jnp.where(top, 0.0, x).astype(BF16)

        def split_across(x):
            return jnp.where(left, x, 0.0).astype(BF16), jnp.where(left, 0.0, x).astype(BF16)

        ids = seg_all[p]
        spread = jnp.broadcast_to(ids, (nz, ROWS, LANES)).reshape(length, LANES)
        seg_col[...] = spread
        seg_row[...] = jnp.transpose(spread)[0:8, :]

        unit, inv = normalize(jnp.transpose(inbuf[p, 0].astype(F32)))
        q_unit[...], q_inv[...] = unit, inv
        low = (unit * q_gain).astype(BF16).astype(F32) * SCALE
        q_t[0], q_t[1] = split_down(low)
        q_n[0], q_n[1] = split_across(jnp.transpose(low))

        unit, inv = normalize(jnp.transpose(inbuf[p, 1].astype(F32)))
        k_unit[...], k_inv[...] = unit, inv
        low = (unit * k_gain).astype(BF16).astype(F32)
        k_t[...] = low.astype(BF16)
        k_n[...] = jnp.transpose(low).astype(BF16)

        v_t[...] = jnp.transpose(inbuf[p, 2].astype(F32)).astype(BF16)
        cot = inbuf[p, 3].astype(F32)
        c_n[0], c_n[1] = split_across(cot)
        c_t[0], c_t[1] = split_down(jnp.transpose(cot))
        key_acc[...] = jnp.zeros_like(key_acc)
        value_acc[...] = jnp.zeros_like(value_acc)

        def step(i, carry):
            at = pl.ds(pl.multiple_of(i * block, block), block)
            wide = jnp.concatenate([seg_col[...]] * (block // LANES), axis=1)
            same = wide == seg_row[0:1, at]
            attended, grad = [], []
            for h in range(2):
                head = pl.ds(h * HEAD_DIM, HEAD_DIM)
                scores = jnp.where(same, dot(k_n[...], q_t[h, :, at]), MASKED)
                exponent = jnp.exp(scores - jnp.max(scores, axis=0, keepdims=True))
                weights = exponent * (1.0 / jnp.sum(exponent, axis=0, keepdims=True))
                weights_low = weights.astype(BF16)
                full = dot(v_t[head, :], weights_low)
                delta = jnp.sum(c_t[h, head, at].astype(F32) * full, axis=0, keepdims=True)
                prob_grad = dot(inbuf[p, 2], c_t[h, :, at])
                score_grad = (weights * (prob_grad - delta)).astype(BF16)
                value_acc[...] += dot(weights_low, c_n[h, at, :])
                key_acc[...] += dot(score_grad, q_n[h, at, :])
                attended.append(full)
                grad.append(dot(k_t[head, :], score_grad) * SCALE)
            outbuf[p, 0, at, :] = jnp.transpose(jnp.concatenate(attended, axis=0)).astype(BF16)
            grad = jnp.concatenate(grad, axis=0)
            unit = q_unit[:, at]
            gain_acc[0] += fold_lanes(grad * unit)
            back = norm_back(grad, unit, q_inv[:, :, at], q_gain)
            outbuf[p, 1, at, :] = jnp.transpose(back).astype(BF16)
            return carry

        lax.fori_loop(0, length // block, step, 0)
        outbuf[p, 3] = value_acc[...].astype(BF16)
        grad = jnp.transpose(key_acc[...])
        unit = k_unit[...]
        gain_acc[1] += fold_lanes(grad * unit)
        back = norm_back(grad, unit, k_inv[...], k_gain)
        outbuf[p, 2] = jnp.transpose(back).astype(BF16)

    for p in range(2):
        arrived(inbuf.at[p], zr.at[p])
        arrived(seg_all.at[p, pl.ds(0, nz - 1)], segr.at[p])
        compute(p)
        send_results(p)

    rows = [jnp.sum(jnp.transpose(gain_acc[i]), axis=0, keepdims=True) for i in range(2)]
    pick = lax.broadcasted_iota(jnp.int32, (8, LANES), 0)
    total = jnp.where(pick == 0, rows[0], jnp.where(pick == 1, rows[1], 0.0))
    for i, group in enumerate(across):
        gain_send[i] = total
        swap = remote(gain_send.at[i], gain_recv.at[i], gs.at[i], gr.at[i], (group, z))
        swap.start()
        swap.wait()
        total = total + gain_recv[i]
    gain_sum[...] = total
    gain_out = pltpu.make_async_copy(gain_sum, gain_ref, load_sem.at[0])
    gain_out.start()

    for p in range(2):
        arrived(ab_ref.at[p], outr.at[p])
        arrived(stage.at[2 * p, :, :, pl.ds(0, lanes - LANES)], zs.at[p])
        arrived(seg_all.at[p, pl.ds(0, nz - 1)], segs.at[p])
        arrived(outbuf.at[p, :, pl.ds(0, length - ROWS), :], outs.at[p])
    gain_out.wait()


def place_kernel(
    moved_hbm, ab_ref, gain_hbm, out0, out1, out2, out3, gq_ref, gk_ref,
    held, moved_ref, gain_ref, gain_low, in_sem, out_sem, small_sem,
):
    moved_in = pltpu.make_async_copy(moved_hbm, moved_ref, small_sem.at[0])
    gain_in = pltpu.make_async_copy(gain_hbm, gain_ref, small_sem.at[1])
    moved_in.start()
    pairs = [(a, p) for p in range(2) for a in range(4)]
    loads = [
        pltpu.make_async_copy(ab_ref.at[p, a], held.at[p, a], in_sem.at[p, a]) for a, p in pairs
    ]
    for load in loads:
        load.start()
    gain_in.start()
    moved_in.wait()
    b_slot = jnp.where(moved_ref[0] == 0, 0, 1)
    outs = (out0, out1, out2, out3)
    stores = []
    for load, (a, p) in zip(loads, pairs):
        slot = 1 - b_slot if p == 0 else b_slot
        load.wait()
        stores.append(
            pltpu.make_async_copy(held.at[p, a], outs[a].at[slot], out_sem.at[p, a])
        )
        stores[-1].start()
    gain_in.wait()
    dp = lax.axis_index("dp")
    lane = lax.broadcasted_iota(jnp.int32, (1, LANES), 1)
    down = lax.broadcasted_iota(jnp.int32, (2, 2), 0)
    across = lax.broadcasted_iota(jnp.int32, (2, 2), 1)
    for i, ref in enumerate((gq_ref, gk_ref)):
        row = gain_ref[i : i + 1, :]
        total = jnp.zeros((2, 2), F32)
        for h in range(2):
            for j in range(2):
                chosen = lane == h * HEAD_DIM + 2 * dp + j
                value = jnp.sum(jnp.where(chosen, row, 0.0), axis=1, keepdims=True)
                total = jnp.where((down == h) & (across == j), value, total)
        gain_low[i] = total
        stores.append(pltpu.make_async_copy(gain_low.at[i], ref, small_sem.at[2 + i]))
        stores[-1].start()
    for store in stores:
        store.wait()


def body(nz, ndp, q, k, v, c, seg, moved, q_gain, k_gain):
    length, lanes = nz * ROWS, nz * LANES
    block = min(256, length)
    hops = ndp.bit_length() - 1
    anywhere = pl.BlockSpec(memory_space=pl.ANY)
    dma = pltpu.SemaphoreType.DMA
    ab, gains = pl.pallas_call(
        functools.partial(main_kernel, nz, ndp, block),
        out_shape=(
            jax.ShapeDtypeStruct((2, 4, ROWS, lanes), BF16),
            jax.ShapeDtypeStruct((8, LANES), F32),
        ),
        in_specs=[anywhere] * 8,
        out_specs=(anywhere, anywhere),
        scratch_shapes=[
            pltpu.VMEM((4, 2, ROWS, lanes), BF16),
            pltpu.SMEM((1,), jnp.int32),
            pltpu.VMEM((2, ROWS), jnp.int32),
            pltpu.VMEM((2, HEAD_DIM), F32),
            pltpu.VMEM((2, HEAD_DIM), F32),
            pltpu.VMEM((3, 4, ROWS, lanes), BF16),
            pltpu.VMEM((4, ROWS, lanes), BF16),
            pltpu.VMEM((2, 4, length, LANES), BF16),
            pltpu.VMEM((2, 4, length, LANES), BF16),
            pltpu.VMEM((3, 1, LANES), F32),
            pltpu.VMEM((1, LANES), F32),
            pltpu.VMEM((2, nz, 1, LANES), F32),
            pltpu.VMEM((LANES, length), F32),
            pltpu.VMEM((LANES, length), F32),
            pltpu.VMEM((2, 1, length), F32),
            pltpu.VMEM((2, 1, length), F32),
            pltpu.VMEM((2, LANES, length), BF16),
            pltpu.VMEM((2, LANES, length), BF16),
            pltpu.VMEM((2, length, LANES), BF16),
            pltpu.VMEM((2, length, LANES), BF16),
            pltpu.VMEM((length, LANES), BF16),
            pltpu.VMEM((LANES, length), BF16),
            pltpu.VMEM((LANES, length), BF16),
            pltpu.VMEM((length, LANES), F32),
            pltpu.VMEM((8, length), F32),
            pltpu.VMEM((length, LANES), F32),
            pltpu.VMEM((length, LANES), F32),
            pltpu.VMEM((2, LANES, LANES), F32),
            pltpu.VMEM((hops, 8, LANES), F32),
            pltpu.VMEM((hops, 8, LANES), F32),
            pltpu.VMEM((8, LANES), F32),
            pltpu.SemaphoreType.REGULAR((max(1, nz // 2 - 1),)),
            dma((8,)),
            dma((4,)), dma((4,)), dma(()), dma(()),
            dma((2,)), dma((2,)), dma((2,)), dma((2,)),
            dma((2,)), dma((2,)), dma((hops,)), dma((hops,)),
        ],
        compiler_params=pltpu.CompilerParams(
            collective_id=0, has_side_effects=True, vmem_limit_bytes=60 << 20
        ),
        name="attend",
    )(moved, q, k, v, c, seg, q_gain, k_gain)
    rows = jax.ShapeDtypeStruct((2, ROWS, lanes), BF16)
    small = jax.ShapeDtypeStruct((2, 2), F32)
    return pl.pallas_call(
        place_kernel,
        out_shape=(rows, rows, rows, rows, small, small),
        in_specs=[anywhere] * 3,
        out_specs=(anywhere,) * 6,
        scratch_shapes=[
            pltpu.VMEM((2, 4, ROWS, lanes), BF16),
            pltpu.SMEM((1,), jnp.int32),
            pltpu.VMEM((8, LANES), F32),
            pltpu.VMEM((2, 2, 2), F32),
            dma((2, 4)), dma((2, 4)), dma((4,)),
        ],
        compiler_params=pltpu.CompilerParams(vmem_limit_bytes=60 << 20),
        name="place",
    )(moved, ab, gains)


def solution(mesh):
    return jax.shard_map(
        functools.partial(body, mesh.shape["seq"], mesh.shape["dp"]),
        mesh=mesh,
        in_specs=(
            P("dp", "seq", None),
            P("dp", "seq", None),
            P("dp", "seq", None),
            P("dp", "seq", None),
            P("dp", "seq"),
            P("dp"),
            P("seq", None),
            P("seq", None),
        ),
        out_specs=(
            P("dp", "seq", None),
            P("dp", "seq", None),
            P("dp", "seq", None),
            P("dp", "seq", None),
            P("seq", "dp"),
            P("seq", "dp"),
        ),
        check_vma=False,
    )
```

```python
import functools

import jax
import jax.numpy as jnp
from jax import lax
from jax.experimental import pallas as pl
from jax.experimental.pallas import tpu as pltpu
from jax.sharding import PartitionSpec as P

MESH = pl.DeviceIdType.MESH
HEAD_DIM = 64
EPSILON = 1e-06
ROWS = 64
LANES = 128
SCALE = HEAD_DIM ** (-0.5)
MASKED = -1e30
F32 = jnp.float32
BF16 = jnp.bfloat16


def dot(a, b):
    return jnp.dot(a, b, preferred_element_type=F32)


def column(gain):
    row = jnp.concatenate([gain[0:1, :], gain[1:2, :]], axis=1)
    return jnp.transpose(jnp.broadcast_to(row, (LANES, LANES)))[:, 0:1]


def normalize(raw):
    parts = raw.reshape(2, HEAD_DIM, raw.shape[1])
    centred = parts - jnp.mean(parts, axis=1, keepdims=True)
    inv_std = lax.rsqrt(jnp.mean(centred * centred, axis=1, keepdims=True) + EPSILON)
    return (centred * inv_std).reshape(raw.shape), inv_std


def norm_back(grad, unit_rows, inv_std, gain):
    scaled = (grad * gain).reshape(2, HEAD_DIM, grad.shape[1])
    unit = unit_rows.reshape(scaled.shape)
    inner = (
        scaled
        - jnp.mean(scaled, axis=1, keepdims=True)
        - unit * jnp.mean(scaled * unit, axis=1, keepdims=True)
    )
    return (inv_std * inner).reshape(grad.shape)


def fold_lanes(x):
    total = x[:, 0:LANES]
    for start in range(LANES, x.shape[1], LANES):
        total = total + x[:, start : start + LANES]
    return total


def main_kernel(
    nz, ndp, block,
    moved_hbm, q_ref, k_ref, v_ref, c_ref, seg_hbm, qg_hbm, kg_hbm,
    ab_ref, gain_ref,
    raw, moved_ref, seg_ref, qg_ref, kg_ref, stage, xrecv, inbuf, outbuf,
    seg_stage, seg_x, seg_all,
    q_unit, k_unit, q_inv, k_inv, q_t, c_t, q_n, c_n, k_n, k_t, v_t, seg_col, seg_row,
    key_acc, value_acc, gain_acc, gain_send, gain_recv, gain_sum,
    known, load_sem, xs, xr, xsegs, xsegr, zs, zr, segs, segr, outs, outr, gs, gr,
):
    dp, z = lax.axis_index("dp"), lax.axis_index("seq")
    length = nz * ROWS
    lanes = nz * LANES
    partner = lax.rem(dp + ndp // 2, ndp)

    def remote(src, dst, send, recv, device):
        return pltpu.make_async_remote_copy(
            src_ref=src, dst_ref=dst, send_sem=send, recv_sem=recv,
            device_id=device, device_id_type=MESH,
        )

    def arrived(ref, sem):
        pltpu.make_async_copy(ref, ref, sem).wait()

    pairs = [(ref, raw.at[a]) for a, ref in enumerate((q_ref, k_ref, v_ref, c_ref))]
    pairs += [(seg_hbm, seg_ref), (qg_hbm, qg_ref), (kg_hbm, kg_ref), (moved_hbm, moved_ref)]
    loads = [
        pltpu.make_async_copy(src, dst, load_sem.at[i]) for i, (src, dst) in enumerate(pairs)
    ]
    by_distance = sorted(range(1, nz), key=lambda d: (-min(d, nz - d), d))

    bits = [1 << i for i in range(ndp.bit_length() - 1)]
    across = [dp + bit * (1 - 2 * lax.rem(dp // bit, 2)) for bit in bits]
    beside = [(dp, lax.rem(z + 1, nz)), (dp, lax.rem(z + nz - 1, nz))]
    barrier = pltpu.get_barrier_semaphore()
    for peer in beside + [(g, z) for g in across]:
        pl.semaphore_signal(barrier, inc=1, device_id=peer, device_id_type=MESH)

    for load in [loads[-1]] + loads[:-1]:
        load.start()

    def tell(k):
        for peer in beside:
            pl.semaphore_signal(known.at[k - 1], inc=1, device_id=peer, device_id_type=MESH)

    def pair(k):
        return [k, nz - k] if k < nz - k else [k]

    def send_rows(p, slot, arrays, distances):
        for d in distances:
            peer = lax.rem(z + d, nz)
            remote(
                stage.at[slot, arrays, :, pl.ds(pl.multiple_of(peer * LANES, LANES), LANES)],
                inbuf.at[p, arrays, pl.ds(pl.multiple_of(z * ROWS, ROWS), ROWS), :],
                zs.at[p], zr.at[p], (dp, peer),
            ).start()

    def keep_rows(p, slot):
        pltpu.make_async_copy(
            stage.at[slot, :, :, pl.ds(pl.multiple_of(z * LANES, LANES), LANES)],
            inbuf.at[p, :, pl.ds(pl.multiple_of(z * ROWS, ROWS), ROWS), :],
            zr.at[p],
        ).start()

    def send_ids():
        seg_all[z] = seg_stage[1]
        for d in by_distance:
            remote(
                seg_stage.at[1], seg_all.at[z], segs, segr, (dp, lax.rem(z + d, nz))
            ).start()

    def send_results(p):
        def put(peer):
            remote(
                outbuf.at[p, :, pl.ds(pl.multiple_of(peer * ROWS, ROWS), ROWS), :],
                ab_ref.at[p, :, :, pl.ds(pl.multiple_of(z * LANES, LANES), LANES)],
                outs.at[p], outr.at[p], (dp, peer),
            ).start()

        first = nz * 7 // 16
        for peer in range(first):

            @pl.when(z != peer)
            def _():
                put(peer)

        for d in by_distance:
            peer = lax.rem(z + d, nz)

            @pl.when(peer >= first)
            def _():
                put(peer)

        pltpu.make_async_copy(
            outbuf.at[p, :, pl.ds(pl.multiple_of(z * ROWS, ROWS), ROWS), :],
            ab_ref.at[p, :, :, pl.ds(pl.multiple_of(z * LANES, LANES), LANES)],
            outr.at[p],
        ).start()

    loads[-1].wait()
    moved = moved_ref[0]
    b_first = moved == 0
    pl.semaphore_wait(barrier, 2 + len(bits))
    far = nz // 2
    if far > 1:
        tell(1)
    for a in range(4):
        loads[a].wait()
        stage[0, a] = jnp.where(b_first, raw[a, 1], raw[a, 0])
        send_rows(0, 0, pl.ds(a, 1), pair(1))
    for k in range(2, far + 1):
        pl.semaphore_wait(known.at[k - 2], 2)
        if k < far:
            tell(k)
        send_rows(0, 0, pl.ds(0, 4), pair(k))
    keep_rows(0, 0)
    trades = []
    for a in range(4):
        stage[1, a] = jnp.where(b_first, raw[a, 0], raw[a, 1])
        trade = remote(stage.at[1, a], xrecv.at[a], xs.at[a], xr.at[a], (partner, z))
        trade.start()
        trades.append(trade)
    for load in loads[4:-1]:
        load.wait()
    segs_in = seg_ref[...].astype(F32)
    seg0 = jnp.broadcast_to(segs_in[0:1, 0:1], (1, LANES))
    seg1 = jnp.broadcast_to(segs_in[1:2, 0:1], (1, LANES))
    seg_a = jnp.where(b_first, seg1, seg0)
    seg_b = jnp.where(b_first, seg0, seg1)
    seg_stage[0] = seg_b
    seg_trade = remote(seg_stage.at[0], seg_x, xsegs, xsegr, (partner, z))
    seg_trade.start()

    stays = moved == 2
    seg_trade.wait()
    half = lax.broadcasted_iota(jnp.int32, (1, LANES), 1) < HEAD_DIM
    seg_stage[1] = jnp.where(half, seg_a, jnp.where(stays, seg_b, seg_x[...]))
    send_ids()
    for a in range(4):
        trades[a].wait()
        stage[2, a] = jnp.where(stays, stage[1, a], xrecv[a])
    send_rows(1, 2, pl.ds(0, 4), by_distance)
    keep_rows(1, 2)

    q_gain, k_gain = column(qg_ref[...]), column(kg_ref[...])
    gain_acc[...] = jnp.zeros_like(gain_acc)

    def compute(p):
        top = lax.broadcasted_iota(jnp.int32, (LANES, length), 0) < HEAD_DIM
        left = lax.broadcasted_iota(jnp.int32, (length, LANES), 1) < HEAD_DIM

        def split_down(x):
            return jnp.where(top, x, 0.0).astype(BF16), jnp.where(top, 0.0, x).astype(BF16)

        def split_across(x):
            return jnp.where(left, x, 0.0).astype(BF16), jnp.where(left, 0.0, x).astype(BF16)

        ids = seg_all[:, :, p * HEAD_DIM : p * HEAD_DIM + 1]
        spread = jnp.broadcast_to(ids, (nz, ROWS, LANES)).reshape(length, LANES)
        seg_col[...] = spread
        seg_row[...] = jnp.transpose(spread)[0:8, :]

        unit, inv = normalize(jnp.transpose(inbuf[p, 0].astype(F32)))
        q_unit[...], q_inv[...] = unit, inv
        low = (unit * q_gain).astype(BF16).astype(F32) * SCALE
        q_t[0], q_t[1] = split_down(low)
        q_n[0], q_n[1] = split_across(jnp.transpose(low))

        unit, inv = normalize(jnp.transpose(inbuf[p, 1].astype(F32)))
        k_unit[...], k_inv[...] = unit, inv
        low = (unit * k_gain).astype(BF16).astype(F32)
        k_t[...] = low.astype(BF16)
        k_n[...] = jnp.transpose(low).astype(BF16)

        v_t[...] = jnp.transpose(inbuf[p, 2].astype(F32)).astype(BF16)
        cot = inbuf[p, 3].astype(F32)
        c_n[0], c_n[1] = split_across(cot)
        c_t[0], c_t[1] = split_down(jnp.transpose(cot))
        key_acc[...] = jnp.zeros_like(key_acc)
        value_acc[...] = jnp.zeros_like(value_acc)

        def step(i, carry):
            at = pl.ds(pl.multiple_of(i * block, block), block)
            wide = jnp.concatenate([seg_col[...]] * (block // LANES), axis=1)
            same = wide == seg_row[0:1, at]
            attended, grad = [], []
            for h in range(2):
                head = pl.ds(h * HEAD_DIM, HEAD_DIM)
                scores = jnp.where(same, dot(k_n[...], q_t[h, :, at]), MASKED)
                exponent = jnp.exp(scores - jnp.max(scores, axis=0, keepdims=True))
                weights = exponent * (1.0 / jnp.sum(exponent, axis=0, keepdims=True))
                weights_low = weights.astype(BF16)
                full = dot(v_t[head, :], weights_low)
                delta = jnp.sum(c_t[h, head, at].astype(F32) * full, axis=0, keepdims=True)
                prob_grad = dot(inbuf[p, 2], c_t[h, :, at])
                score_grad = (weights * (prob_grad - delta)).astype(BF16)
                value_acc[...] += dot(weights_low, c_n[h, at, :])
                key_acc[...] += dot(score_grad, q_n[h, at, :])
                attended.append(full)
                grad.append(dot(k_t[head, :], score_grad) * SCALE)
            outbuf[p, 0, at, :] = jnp.transpose(jnp.concatenate(attended, axis=0)).astype(BF16)
            grad = jnp.concatenate(grad, axis=0)
            unit = q_unit[:, at]
            gain_acc[0] += fold_lanes(grad * unit)
            back = norm_back(grad, unit, q_inv[:, :, at], q_gain)
            outbuf[p, 1, at, :] = jnp.transpose(back).astype(BF16)
            return carry

        lax.fori_loop(0, length // block, step, 0)
        outbuf[p, 3] = value_acc[...].astype(BF16)
        grad = jnp.transpose(key_acc[...])
        unit = k_unit[...]
        gain_acc[1] += fold_lanes(grad * unit)
        back = norm_back(grad, unit, k_inv[...], k_gain)
        outbuf[p, 2] = jnp.transpose(back).astype(BF16)

    for p in range(2):
        arrived(inbuf.at[p], zr.at[p])
        if p == 0:
            arrived(seg_all.at[pl.ds(0, nz - 1)], segr)
        compute(p)
        send_results(p)

    rows = [jnp.sum(jnp.transpose(gain_acc[i]), axis=0, keepdims=True) for i in range(2)]
    pick = lax.broadcasted_iota(jnp.int32, (8, LANES), 0)
    total = jnp.where(pick == 0, rows[0], jnp.where(pick == 1, rows[1], 0.0))
    for i, group in enumerate(across):
        gain_send[i] = total
        swap = remote(gain_send.at[i], gain_recv.at[i], gs.at[i], gr.at[i], (group, z))
        swap.start()
        swap.wait()
        total = total + gain_recv[i]
    gain_sum[...] = total
    gain_out = pltpu.make_async_copy(gain_sum, gain_ref, load_sem.at[0])
    gain_out.start()

    for p in range(2):
        arrived(ab_ref.at[p], outr.at[p])
        arrived(stage.at[2 * p, :, :, pl.ds(0, lanes - LANES)], zs.at[p])
        arrived(outbuf.at[p, :, pl.ds(0, length - ROWS), :], outs.at[p])
    arrived(seg_all.at[pl.ds(0, nz - 1)], segs)
    gain_out.wait()


def place_kernel(
    moved_hbm, ab_ref, gain_hbm, out0, out1, out2, out3, gq_ref, gk_ref,
    held, moved_ref, gain_ref, gain_low, in_sem, out_sem, small_sem,
):
    moved_in = pltpu.make_async_copy(moved_hbm, moved_ref, small_sem.at[0])
    gain_in = pltpu.make_async_copy(gain_hbm, gain_ref, small_sem.at[1])
    moved_in.start()
    pairs = [(a, p) for p in range(2) for a in range(4)]
    loads = [
        pltpu.make_async_copy(ab_ref.at[p, a], held.at[p, a], in_sem.at[p, a]) for a, p in pairs
    ]
    for load in loads:
        load.start()
    gain_in.start()
    moved_in.wait()
    b_slot = jnp.where(moved_ref[0] == 0, 0, 1)
    outs = (out0, out1, out2, out3)
    stores = []
    for load, (a, p) in zip(loads, pairs):
        slot = 1 - b_slot if p == 0 else b_slot
        load.wait()
        stores.append(
            pltpu.make_async_copy(held.at[p, a], outs[a].at[slot], out_sem.at[p, a])
        )
        stores[-1].start()
    gain_in.wait()
    dp = lax.axis_index("dp")
    lane = lax.broadcasted_iota(jnp.int32, (1, LANES), 1)
    down = lax.broadcasted_iota(jnp.int32, (2, 2), 0)
    across = lax.broadcasted_iota(jnp.int32, (2, 2), 1)
    for i, ref in enumerate((gq_ref, gk_ref)):
        row = gain_ref[i : i + 1, :]
        total = jnp.zeros((2, 2), F32)
        for h in range(2):
            for j in range(2):
                chosen = lane == h * HEAD_DIM + 2 * dp + j
                value = jnp.sum(jnp.where(chosen, row, 0.0), axis=1, keepdims=True)
                total = jnp.where((down == h) & (across == j), value, total)
        gain_low[i] = total
        stores.append(pltpu.make_async_copy(gain_low.at[i], ref, small_sem.at[2 + i]))
        stores[-1].start()
    for store in stores:
        store.wait()


def body(nz, ndp, q, k, v, c, seg, moved, q_gain, k_gain):
    length, lanes = nz * ROWS, nz * LANES
    block = min(256, length)
    hops = ndp.bit_length() - 1
    anywhere = pl.BlockSpec(memory_space=pl.ANY)
    dma = pltpu.SemaphoreType.DMA
    ab, gains = pl.pallas_call(
        functools.partial(main_kernel, nz, ndp, block),
        out_shape=(
            jax.ShapeDtypeStruct((2, 4, ROWS, lanes), BF16),
            jax.ShapeDtypeStruct((8, LANES), F32),
        ),
        in_specs=[anywhere] * 8,
        out_specs=(anywhere, anywhere),
        scratch_shapes=[
            pltpu.VMEM((4, 2, ROWS, lanes), BF16),
            pltpu.SMEM((1,), jnp.int32),
            pltpu.VMEM((2, ROWS), jnp.int32),
            pltpu.VMEM((2, HEAD_DIM), F32),
            pltpu.VMEM((2, HEAD_DIM), F32),
            pltpu.VMEM((3, 4, ROWS, lanes), BF16),
            pltpu.VMEM((4, ROWS, lanes), BF16),
            pltpu.VMEM((2, 4, length, LANES), BF16),
            pltpu.VMEM((2, 4, length, LANES), BF16),
            pltpu.VMEM((2, 1, LANES), F32),
            pltpu.VMEM((1, LANES), F32),
            pltpu.VMEM((nz, 1, LANES), F32),
            pltpu.VMEM((LANES, length), F32),
            pltpu.VMEM((LANES, length), F32),
            pltpu.VMEM((2, 1, length), F32),
            pltpu.VMEM((2, 1, length), F32),
            pltpu.VMEM((2, LANES, length), BF16),
            pltpu.VMEM((2, LANES, length), BF16),
            pltpu.VMEM((2, length, LANES), BF16),
            pltpu.VMEM((2, length, LANES), BF16),
            pltpu.VMEM((length, LANES), BF16),
            pltpu.VMEM((LANES, length), BF16),
            pltpu.VMEM((LANES, length), BF16),
            pltpu.VMEM((length, LANES), F32),
            pltpu.VMEM((8, length), F32),
            pltpu.VMEM((length, LANES), F32),
            pltpu.VMEM((length, LANES), F32),
            pltpu.VMEM((2, LANES, LANES), F32),
            pltpu.VMEM((hops, 8, LANES), F32),
            pltpu.VMEM((hops, 8, LANES), F32),
            pltpu.VMEM((8, LANES), F32),
            pltpu.SemaphoreType.REGULAR((max(1, nz // 2 - 1),)),
            dma((8,)),
            dma((4,)), dma((4,)), dma(()), dma(()),
            dma((2,)), dma((2,)), dma(()), dma(()),
            dma((2,)), dma((2,)), dma((hops,)), dma((hops,)),
        ],
        compiler_params=pltpu.CompilerParams(
            collective_id=0, has_side_effects=True, vmem_limit_bytes=60 << 20
        ),
        name="attend",
    )(moved, q, k, v, c, seg, q_gain, k_gain)
    rows = jax.ShapeDtypeStruct((2, ROWS, lanes), BF16)
    small = jax.ShapeDtypeStruct((2, 2), F32)
    return pl.pallas_call(
        place_kernel,
        out_shape=(rows, rows, rows, rows, small, small),
        in_specs=[anywhere] * 3,
        out_specs=(anywhere,) * 6,
        scratch_shapes=[
            pltpu.VMEM((2, 4, ROWS, lanes), BF16),
            pltpu.SMEM((1,), jnp.int32),
            pltpu.VMEM((8, LANES), F32),
            pltpu.VMEM((2, 2, 2), F32),
            dma((2, 4)), dma((2, 4)), dma((4,)),
        ],
        compiler_params=pltpu.CompilerParams(vmem_limit_bytes=60 << 20),
        name="place",
    )(moved, ab, gains)


def solution(mesh):
    return jax.shard_map(
        functools.partial(body, mesh.shape["seq"], mesh.shape["dp"]),
        mesh=mesh,
        in_specs=(
            P("dp", "seq", None),
            P("dp", "seq", None),
            P("dp", "seq", None),
            P("dp", "seq", None),
            P("dp", "seq"),
            P("dp"),
            P("seq", None),
            P("seq", None),
        ),
        out_specs=(
            P("dp", "seq", None),
            P("dp", "seq", None),
            P("dp", "seq", None),
            P("dp", "seq", None),
            P("seq", "dp"),
            P("seq", "dp"),
        ),
        check_vma=False,
    )
```
